256 devices in a mesh: dom: 16 (over x, z_hi), col: 16 (over y, z_lo, core).
Axes of the slice: x: 4, y: 4, z: 8 (z_hi: 4, z_lo: 2; z = z_hi * 2 + z_lo), core: 2. Of those that a mesh axis runs over, the one named last changes fastest.
Arguments:
- features: float32 [32768, 1024], P('dom', 'col'), may hold values from -6 to 6
- neighbours: int32 [128, 7], replicated, may hold values from 0 to 127, as said below
- tiles: bfloat16 [128, 8, 256, 256], P('dom'), may hold values from -0.125 to 0.125
- weight: float32 [1024, 1024], P(None, 'col'), may hold values from -0.1875 to 0.1875
- cotangent: float32 [32768, 1024], P('dom', 'col'), may hold values from -6 to 6
Outputs:
- hidden: float32 [32768, 1024], P('dom', 'col')
- grad_features: float32 [32768, 1024], P('dom', 'col')
- grad_weight: float32 [1024, 1024], P('dom', 'col')
The draws below stay inside these ranges and needn't reach their ends.
Inputs may be any that keep to these rules, and one draw needn't show every extreme that they name: `neighbours`: row blocks i of one index of dom are i from d * 8 to (d + 1) * 8 - 1 for index d, which also holds those node blocks. No entry of a row block names a block of its own index of dom, and the row blocks of one index of dom name blocks of any one other index at most 4 times in all, counting repeats; that many is reached in every draw.
All inputs are finite; a program needn't handle non-finite values.
Results may differ from the reference program's by a relative error of at most 0.0003.
Values sent between devices are 32-bit elements; how exact they have to be, the bound alone decides.
No kernel may reach another device: no remote copies, remote signals or barrier semaphores. Data moves between devices by JAX's collectives and lax.ppermute only.
A program may use at most 128 MiB of HBM per device.

```python
import jax
import jax.numpy as jnp
from jax import lax

F = 1024
B = 256
BLK_DEV = 8
K = 8
NBLK = 128
NODES = 32768


def draw_neighbours(key, part):
    key = jax.random.fold_in(key, 17)
    groups = NBLK // BLK_DEV
    refs = BLK_DEV * (K - 1)
    slots = max(4, (refs + groups - 2) // (groups - 1))
    keys = jax.random.split(jax.random.fold_in(key, 1), groups)
    orders = jax.vmap(lambda single: jax.random.permutation(single, groups - 1))(keys)
    offset = orders[:, jnp.arange(refs) // slots]
    sender = (jnp.arange(groups)[:, None] + 1 + offset) % groups
    inside = jax.random.randint(jax.random.fold_in(key, 2), (groups, refs), 0, BLK_DEV)
    return (sender * BLK_DEV + inside).reshape(NBLK, K - 1).astype(jnp.int32)


def levels(own_key, shape, cuts, least, top_value):
    level, own = 1.0, jax.random.fold_in(own_key, 6)
    for dim, parts in cuts:
        steps = jnp.exp(jax.random.uniform(jax.random.fold_in(own, dim), (parts,), jnp.float32, least / len(cuts), top_value / len(cuts)))
        level = level * jnp.repeat(steps, shape[dim] // parts).reshape([-1 if axis == dim else 1 for axis in range(len(shape))])
    return level


def normal_values(own_key, dims, width, most, cuts=(), kind=jnp.bfloat16):
    entries = jax.random.normal(own_key, dims, jnp.float32) * width
    if len(cuts) > 0:
        entries = levels(own_key, dims, cuts, -0.22, 0.18) * entries
    return jnp.clip(entries, min=-most, max=most).astype(kind)


def setup_inputs(seed: int = 0) -> dict:
    key_of = jax.random.split(jax.random.key(seed), 6)
    return {
        "features": normal_values(key_of[0], (NODES, F), 1.0, 6.0, ((0, 16), (1, 16)), jnp.float32),
        "neighbours": draw_neighbours(jax.random.fold_in(key_of[5], 71), 0),
        "tiles": normal_values(key_of[2], (NBLK, K, B, B), (K * B) ** -0.5, 0.125, ((0, 16),)),
        "weight": normal_values(key_of[3], (F, F), F ** -0.5, 0.1875, ((1, 16),), jnp.float32),
        "cotangent": normal_values(key_of[4], (NODES, F), 1.0, 6.0, ((0, 16), (1, 16)), jnp.float32),
    }


def reference(features, neighbours, tiles, weight, cotangent):
    highest = lax.Precision.HIGHEST
    blocks = features.reshape(NBLK, B, F)

    def row_block(index):
        targets = jnp.concatenate([index[None], neighbours[index]]).astype(jnp.int32)
        picked = blocks[targets]
        return jnp.einsum("kab,kbc->ac", tiles[index].astype(jnp.float32), picked, precision=highest)

    mixed = lax.map(row_block, jnp.arange(NBLK, dtype=jnp.int32)).reshape(NODES, F)
    pre = jnp.dot(mixed, weight, precision=highest)
    sig = jax.nn.sigmoid(pre)
    hidden = pre * sig
    slope = cotangent * sig * (1.0 + pre * (1.0 - sig))
    grad_weight = jnp.dot(mixed.T, slope, precision=highest)
    back = jnp.dot(slope, weight.T, precision=highest).reshape(NBLK, B, F)

    def push(total, index):
        contrib = jnp.einsum("kab,ac->kbc", tiles[index].astype(jnp.float32), back[index], precision=highest)
        targets = jnp.concatenate([index[None], neighbours[index]]).astype(jnp.int32)
        return total.at[targets].add(contrib), None

    start = jnp.zeros((NBLK, B, F), jnp.float32)
    total, unused = lax.scan(push, start, jnp.arange(NBLK, dtype=jnp.int32))
    return hidden, total.reshape(NODES, F), grad_weight
```

```python
import functools

import jax
import jax.numpy as jnp
from jax import lax
from jax.experimental import pallas as pl
from jax.experimental.pallas import tpu as pltpu
from jax.sharding import Mesh
from jax.sharding import PartitionSpec as P

DOM = ("x", "zh")
COL = ("y", "zl", "c")
NX, NZ, NY = 4, 4, 4
BLK, FAN, W, C = 8, 8, 256, 64
REFS = BLK * (FAN - 1)
SLOTS = 4
F = 1024
CHUNK = 128
f32, bf16 = jnp.float32, jnp.bfloat16
VMEM = pl.BlockSpec(memory_space=pltpu.VMEM)
SMEM = pl.BlockSpec(memory_space=pltpu.SMEM)
ANY = pl.BlockSpec(memory_space=pl.ANY)
PARAMS = pltpu.CompilerParams(vmem_limit_bytes=40 * 2**20)


def split(value):
    hi = value.astype(bf16)
    lo = (value - hi.astype(f32)).astype(bf16)
    return hi, lo


def tables(neighbours):
    me_x, me_z = lax.axis_index("x"), lax.axis_index("zh")
    rows = neighbours.reshape(NX, NZ, REFS)
    rows = lax.dynamic_index_in_dim(rows, me_z, 1, keepdims=False)
    owner, block = rows >> 3, rows & 7
    ref = jnp.arange(REFS)
    same = (owner[:, :, None] == owner[:, None, :]) & (ref[None, :, None] > ref[None, None, :])
    rank = jnp.sum(same.astype(jnp.int32), axis=2)
    wanted = me_x * NZ + ((me_z + jnp.arange(NZ)) & (NZ - 1))
    match = (owner[None, :, None, :] == wanted[:, None, None, None]) & (
        rank[None, :, None, :] == jnp.arange(SLOTS)[None, None, :, None]
    )
    table = jnp.sum(jnp.where(match, block[None, :, None, :] + 1, 0), axis=3)
    mine = lax.dynamic_index_in_dim(owner, me_x, 0, keepdims=False)
    my_rank = lax.dynamic_index_in_dim(rank, me_x, 0, keepdims=False)
    e, xs = ((mine & 3) - me_z) & 3, mine >> 2
    start = jnp.where(e == 0, 0, jnp.where(e == 2, 48, 16 + (e >> 1) * 4))
    stride = jnp.where((e & 1) == 1, 8, 4)
    where_ = start + xs * stride + my_rank
    near = table[0].reshape(16)
    mid = jnp.stack([table[1], table[3]], axis=1).reshape(32)
    far = table[2].reshape(16)
    return near, mid, far, jnp.clip(where_, 0, 63)


def pick_kernel(count, index_ref, *refs):
    sources, out, sems = refs[:count], refs[count], refs[count + 1]
    total = out.shape[0]
    copies = []
    for slot in range(total):
        source = sources[(slot // SLOTS) % count]
        index = jnp.clip(index_ref[slot] - 1, 0, BLK - 1)
        copies.append(pltpu.make_async_copy(source.at[index], out.at[slot], sems.at[slot]))
    for copy in copies:
        copy.start()
    for copy in copies:
        copy.wait()


def pick(index, *sources):
    total = NX * SLOTS * len(sources)
    return pl.pallas_call(
        functools.partial(pick_kernel, len(sources)),
        out_shape=jax.ShapeDtypeStruct((total, C, W), f32),
        in_specs=[SMEM] + [ANY] * len(sources),
        out_specs=ANY,
        scratch_shapes=[pltpu.SemaphoreType.DMA((total,))],
        cost_estimate=pl.CostEstimate(flops=0, bytes_accessed=total * C * W * 8, transcendentals=0),
    )(index, *sources)


def mixed_kernel(where_ref, own_ref, near_ref, mid_ref, far_ref, tiles_ref, out_ref, held, sems):
    i = pl.program_id(0)

    @pl.when(i == 0)
    def _():
        copies = [
            pltpu.make_async_copy(near_ref, held.at[pl.ds(0, 16)], sems.at[0]),
            pltpu.make_async_copy(mid_ref, held.at[pl.ds(16, 32)], sems.at[1]),
            pltpu.make_async_copy(far_ref, held.at[pl.ds(48, 16)], sems.at[2]),
        ]
        for copy in copies:
            copy.start()
        for copy in copies:
            copy.wait()

    acc = None
    for k in range(FAN):
        block = own_ref[0] if k == 0 else held[where_ref[i * (FAN - 1) + k - 1]]
        part = lax.dot_general(
            jnp.concatenate(split(block), axis=0),
            tiles_ref[0, k],
            (((1,), (1,)), ((), ())),
            preferred_element_type=f32,
        )
        acc = part if acc is None else acc + part
    value = acc[:C] + acc[C:]
    out_ref[0] = value[:, :CHUNK]
    out_ref[1] = value[:, CHUNK:]


def mix(where_, own, near, mid, far, tiles):
    return pl.pallas_call(
        mixed_kernel,
        grid_spec=pltpu.PrefetchScalarGridSpec(
            num_scalar_prefetch=1,
            grid=(BLK,),
            in_specs=[
                pl.BlockSpec((1, C, W), lambda i, s: (i, 0, 0)),
                ANY,
                ANY,
                ANY,
                pl.BlockSpec((1, FAN, W, W), lambda i, s: (i, 0, 0, 0)),
            ],
            out_specs=pl.BlockSpec((2, C, CHUNK), lambda i, s: (i, 0, 0)),
            scratch_shapes=[pltpu.VMEM((64, C, W), f32), pltpu.SemaphoreType.DMA((3,))],
        ),
        out_shape=jax.ShapeDtypeStruct((16, C, CHUNK), f32),
        compiler_params=PARAMS,
        cost_estimate=pl.CostEstimate(flops=2 * 64 * W * W * 2 * C, bytes_accessed=13 << 20, transcendentals=0),
    )(where_, own, near, mid, far, tiles)


def weight_kernel(in_ref, thi_ref, tlo_ref, hi_ref, lo_ref):
    value = in_ref[...]
    thi_ref[...], tlo_ref[...] = split(value)
    hi_ref[...], lo_ref[...] = split(value.T)


def weight_parts(transposed):
    step = 256
    by_row = pl.BlockSpec((step, F), lambda i: (i, 0))
    by_col = pl.BlockSpec((F, step), lambda i: (0, i))
    return pl.pallas_call(
        weight_kernel,
        grid=(F // step,),
        in_specs=[by_row],
        out_specs=[by_row, by_row, by_col, by_col],
        out_shape=[jax.ShapeDtypeStruct((F, F), bf16)] * 4,
        compiler_params=PARAMS,
        cost_estimate=pl.CostEstimate(flops=F * F * 8, bytes_accessed=12 << 20, transcendentals=0),
    )(transposed)


def dense_kernel(thi_ref, tlo_ref, hi_ref, lo_ref, mixed_ref, cot_ref, hidden_ref, slope_ref, back_ref, parts):
    step = pl.program_id(0)

    @pl.when(step == 0)
    def _():
        hi, lo = split(mixed_ref[...])
        parts[:, :CHUNK] = hi
        parts[:, CHUNK:] = lo

    both = jnp.dot(thi_ref[...], parts[...], preferred_element_type=f32)
    low = jnp.dot(tlo_ref[...], parts[:, :CHUNK], preferred_element_type=f32)
    pre = both[:, :CHUNK] + (both[:, CHUNK:] + low)
    sig = jax.nn.sigmoid(pre)
    hidden_ref[...] = pre * sig
    slope = cot_ref[...] * sig * (1.0 + pre * (1.0 - sig))
    slope_ref[...] = slope
    shi, slo = split(slope)
    both = jnp.dot(hi_ref[...], jnp.concatenate([shi, slo], axis=1), preferred_element_type=f32)
    low = jnp.dot(lo_ref[...], shi, preferred_element_type=f32)
    part = both[:, :CHUNK] + (both[:, CHUNK:] + low)

    @pl.when(step == 0)
    def _():
        back_ref[...] = part

    @pl.when(step > 0)
    def _():
        back_ref[...] += part


def dense(weights, mixed, cot):
    step = 256
    by_row = pl.BlockSpec((step, F), lambda i: (i, 0))
    by_col = pl.BlockSpec((F, step), lambda i: (0, i))
    rows = pl.BlockSpec((step, CHUNK), lambda i: (i, 0))
    whole = pl.BlockSpec((F, CHUNK), lambda i: (0, 0))
    return pl.pallas_call(
        dense_kernel,
        grid=(F // step,),
        in_specs=[by_row, by_row, by_col, by_col, whole, rows],
        out_specs=[rows, rows, whole],
        out_shape=[jax.ShapeDtypeStruct((F, CHUNK), f32)] * 3,
        scratch_shapes=[pltpu.VMEM((F, 2 * CHUNK), bf16)],
        compiler_params=PARAMS,
        cost_estimate=pl.CostEstimate(flops=12 * F * F * CHUNK, bytes_accessed=10 << 20, transcendentals=F * CHUNK),
    )(*weights, mixed, cot)


def push_kernel(where_ref, back_ref, tiles_ref, diag_ref, near_ref, mid_ref, far_ref, held, sems):
    i = pl.program_id(0)
    block = jnp.concatenate([back_ref[0], back_ref[1]], axis=1)
    both = jnp.concatenate(split(block), axis=0)
    for k in range(FAN):
        part = jnp.dot(both, tiles_ref[0, k], preferred_element_type=f32)
        value = part[:C] + part[C:]
        if k == 0:
            diag_ref[0] = value
        else:
            held[where_ref[i * (FAN - 1) + k - 1]] = value

    @pl.when(i == BLK - 1)
    def _():
        copies = [
            pltpu.make_async_copy(held.at[pl.ds(48, 16)], far_ref, sems.at[0]),
            pltpu.make_async_copy(held.at[pl.ds(16, 32)], mid_ref, sems.at[1]),
            pltpu.make_async_copy(held.at[pl.ds(0, 16)], near_ref, sems.at[2]),
        ]
        for copy in copies:
            copy.start()
        for copy in copies:
            copy.wait()


def push(where_, back, tiles):
    return pl.pallas_call(
        push_kernel,
        grid_spec=pltpu.PrefetchScalarGridSpec(
            num_scalar_prefetch=1,
            grid=(BLK,),
            in_specs=[
                pl.BlockSpec((2, C, CHUNK), lambda i, s: (i, 0, 0)),
                pl.BlockSpec((1, FAN, W, W), lambda i, s: (i, 0, 0, 0)),
            ],
            out_specs=[pl.BlockSpec((1, C, W), lambda i, s: (i, 0, 0)), ANY, ANY, ANY],
            scratch_shapes=[pltpu.VMEM((64, C, W), f32), pltpu.SemaphoreType.DMA((3,))],
        ),
        out_shape=[jax.ShapeDtypeStruct((n, C, W), f32) for n in (BLK, 16, 32, 16)],
        compiler_params=PARAMS,
        cost_estimate=pl.CostEstimate(flops=2 * 64 * W * W * 2 * C, bytes_accessed=13 << 20, transcendentals=0),
    )(where_, back, tiles)


def gather_sum_kernel(slots, first, last, index_ref, *refs):
    got_ref, out_ref = refs[0], refs[-1]
    start = refs[1] if len(refs) == 3 else None
    for block in range(BLK):
        if first <= block < last:
            out_ref[block] = start[block - first]
        else:
            out_ref[block] = jnp.zeros((C, W), f32)
    for slot in slots:
        index = index_ref[slot]

        @pl.when(index > 0)
        def _():
            out_ref[index - 1] += got_ref[slot]


def gather_sum(index, got, slots, start=None, first=0):
    last = first if start is None else first + start.shape[0]
    args = (index, got) if start is None else (index, got, start)
    return pl.pallas_call(
        functools.partial(gather_sum_kernel, slots, first, last),
        out_shape=jax.ShapeDtypeStruct((BLK, C, W), f32),
        in_specs=[SMEM] + [VMEM] * (len(args) - 1),
        out_specs=VMEM,
        compiler_params=PARAMS,
        cost_estimate=pl.CostEstimate(flops=16 * C * W, bytes_accessed=3 << 20, transcendentals=0),
    )(*args)


def shift(value, axis, size, by):
    return lax.ppermute(value, axis, [(i, (i + by) % size) for i in range(size)])


def over_x(value):
    count = value.shape[0] // NX
    out = lax.all_to_all(value.reshape(NX, count, C, W), "x", 0, 0, tiled=True)
    return out.reshape(value.shape)


def over_col(value):
    return lax.all_to_all(value, COL, 0, 0, tiled=True)


def on_device(features, neighbours, tiles, weight, cotangent):
    near_at, mid_at, far_at, where_ = tables(neighbours)
    own = features.T.reshape(C, BLK, W).transpose(1, 0, 2)

    up = shift(own, "zh", NZ, -1)
    down = shift(own, "zh", NZ, 1)
    near = over_x(pick(near_at, own))
    weights = weight_parts(lax.all_gather(weight.T, COL, axis=0, tiled=True))
    cot = over_col(cotangent.T.reshape(C, 16, CHUNK).transpose(1, 0, 2)).reshape(F, CHUNK)
    far_lo = shift(up[: BLK // 2], "zh", NZ, -1)
    far_hi = shift(down[BLK // 2 :], "zh", NZ, 1)
    mid = over_x(pick(mid_at, up, down))
    far = over_x(pick(far_at, jnp.concatenate([far_lo, far_hi], axis=0)))
    mixed = mix(where_, own, near, mid, far, tiles)

    mixed = over_col(mixed).reshape(F, CHUNK)
    hidden, slope, back = dense(weights, mixed, cot)
    back = over_col(back.reshape(16, C, CHUNK))
    hidden = over_col(hidden.reshape(16, C, CHUNK)).transpose(1, 0, 2).reshape(C, 16 * CHUNK).T

    diag, near, mid, far = push(where_, back, tiles)
    far = gather_sum(far_at, over_x(far), range(16))
    from_below = shift(far[: BLK // 2], "zh", NZ, 1)
    from_above = shift(far[BLK // 2 :], "zh", NZ, -1)
    mid = over_x(mid)
    up = gather_sum(mid_at, mid, [s for s in range(32) if s % 8 < 4], from_below, 0)
    down = gather_sum(mid_at, mid, [s for s in range(32) if s % 8 >= 4], from_above, BLK // 2)
    up = shift(up, "zh", NZ, 1)
    down = shift(down, "zh", NZ, -1)
    near = gather_sum(near_at, over_x(near), range(16), diag, 0)
    grad_features = (near + up + down).transpose(1, 0, 2).reshape(C, BLK * W).T

    me_c, me_l = lax.axis_index("c"), lax.axis_index("zl")
    by_core = slope.reshape(8, 2, C, CHUNK)

    def partial(core):
        rows = lax.dynamic_index_in_dim(by_core, core, 1, keepdims=False).reshape(8 * C, CHUNK)
        return lax.dot_general(
            rows, mixed, (((1,), (1,)), ((), ())), precision=lax.Precision.HIGH, preferred_element_type=f32
        )

    grad = partial(me_c) + shift(partial(1 - me_c), "c", 2, 1)
    grad = lax.all_to_all(grad.reshape(NY, 2 * C, F), "y", 0, 0, tiled=True).sum(axis=0).reshape(2, C, F)
    other = shift(lax.dynamic_index_in_dim(grad, 1 - me_l, 0, keepdims=False), "zl", 2, 1)
    grad = lax.dynamic_index_in_dim(grad, me_l, 0, keepdims=False) + other
    grad = grad.reshape(2, C // 2, 16, C).transpose(2, 1, 0, 3).reshape(16, C // 2, 2 * C)
    grad = lax.all_to_all(grad, DOM, 0, 0, tiled=True).sum(axis=0)
    grad_weight = grad.reshape(C // 2, 2, C).transpose(1, 0, 2).reshape(C, C).T
    return hidden, grad_features, grad_weight


def solution(mesh):
    fine = Mesh(mesh.devices.reshape(4, 4, 4, 2, 2), DOM + COL)
    in_specs = (P(DOM, COL), P(), P(DOM, None, None, None), P(None, COL), P(DOM, COL))
    out_specs = (P(DOM, COL), P(DOM, COL), P(DOM, COL))
    return jax.shard_map(on_device, mesh=fine, in_specs=in_specs, out_specs=out_specs, check_vma=False)
```

```python
import functools

import jax
import jax.numpy as jnp
from jax import lax
from jax.experimental import pallas as pl
from jax.experimental.pallas import tpu as pltpu
from jax.sharding import Mesh
from jax.sharding import PartitionSpec as P

DOM = ("x", "zh")
COL = ("y", "zl", "c")
NX, NZ, NY = 4, 4, 4
BLK, FAN, W, C = 8, 8, 256, 64
REFS = BLK * (FAN - 1)
SLOTS = 4
HELD = 72
F = 1024
CHUNK = 128
f32, bf16 = jnp.float32, jnp.bfloat16
VMEM = pl.BlockSpec(memory_space=pltpu.VMEM)
SMEM = pl.BlockSpec(memory_space=pltpu.SMEM)
ANY = pl.BlockSpec(memory_space=pl.ANY)
PARAMS = pltpu.CompilerParams(vmem_limit_bytes=58 * 2**20)


def split(value):
    hi = value.astype(bf16)
    lo = (value - hi.astype(f32)).astype(bf16)
    return hi, lo


def tables(neighbours):
    me_x, me_z = lax.axis_index("x"), lax.axis_index("zh")
    rows = neighbours.reshape(NX, NZ, REFS)
    rows = lax.dynamic_index_in_dim(rows, me_z, 1, keepdims=False)
    rows = lax.dynamic_slice_in_dim(jnp.concatenate([rows, rows], axis=0), me_x, NX, 0)
    owner, block = rows >> 3, rows & 7
    ref = jnp.arange(REFS)
    same = (owner[:, :, None] == owner[:, None, :]) & (ref[None, :, None] > ref[None, None, :])
    rank = jnp.sum(same.astype(jnp.int32), axis=2)
    wanted = me_x * NZ + ((me_z + jnp.arange(NZ)) & (NZ - 1))
    match = (owner[None, 1:, None, :] == wanted[:, None, None, None]) & (
        rank[None, 1:, None, :] == jnp.arange(SLOTS)[None, None, :, None]
    )
    table = jnp.sum(jnp.where(match, block[None, 1:, None, :] + 1, 0), axis=3)
    e, s = ((owner[0] & 3) - me_z) & 3, (me_x - (owner[0] >> 2)) & 3
    local = jnp.where(e == 2, 0, jnp.where(e == 1, 8, 16)) + block[0]
    start = jnp.where(e == 0, 24, jnp.where(e == 2, 60, 36 + (e >> 1) * 4))
    stride = jnp.where((e & 1) == 1, 8, 4)
    place = jnp.where(s == 0, local, start + (s - 1) * stride + rank[0])
    near = table[0].reshape(12)
    mid = jnp.stack([table[1], table[3]], axis=1).reshape(24)
    far = table[2].reshape(12)
    return near, mid, far, jnp.clip(place, 0, HELD - 1)


def pick_kernel(index_ref, *refs):
    sources, outs = refs[:-3], refs[-3:]
    per = outs[0].shape[0]
    for s in range(3):
        for slot in range(per):
            index = jnp.maximum(index_ref[s * per + slot] - 1, 0)
            outs[s][slot] = sources[slot // SLOTS][index]


def pick_halves_kernel(index_ref, lo_ref, hi_ref, *refs):
    outs, held = refs[:3], refs[3]
    held[: BLK // 2] = lo_ref[...]
    held[BLK // 2 :] = hi_ref[...]
    pick_kernel(index_ref, held, *outs)


def pick(index, *sources, halves=False):
    per = SLOTS * (1 if halves else len(sources))
    return pl.pallas_call(
        pick_halves_kernel if halves else pick_kernel,
        out_shape=[jax.ShapeDtypeStruct((per, C, W), f32)] * 3,
        in_specs=[SMEM] + [VMEM] * len(sources),
        out_specs=[VMEM] * 3,
        scratch_shapes=[pltpu.VMEM((BLK, C, W), f32)] if halves else [],
        compiler_params=PARAMS,
        cost_estimate=pl.CostEstimate(flops=0, bytes_accessed=per * C * W * 24, transcendentals=0),
    )(index, *sources)


def places(refs):
    start, pairs = 0, []
    for ref in refs:
        pairs.append((pl.ds(start, ref.shape[0]), ref))
        start += ref.shape[0]
    return pairs


def mixed_kernel(place_ref, own_ref, *refs):
    sources, tiles_ref, out_ref, held, sems = refs[:13], *refs[13:]
    i = pl.program_id(0)

    @pl.when(i == 0)
    def _():
        copies = [
            pltpu.make_async_copy(ref, held.at[rows], sems.at[n]) for n, (rows, ref) in enumerate(places(sources))
        ]
        for copy in copies:
            copy.start()
        for copy in copies:
            copy.wait()

    acc = None
    for k in range(FAN):
        block = own_ref[0] if k == 0 else held[place_ref[i * (FAN - 1) + k - 1]]
        part = lax.dot_general(
            jnp.concatenate(split(block), axis=0),
            tiles_ref[0, k],
            (((1,), (1,)), ((), ())),
            preferred_element_type=f32,
        )
        acc = part if acc is None else acc + part
    value = acc[:C] + acc[C:]
    out_ref[0] = value[:, :CHUNK]
    out_ref[1] = value[:, CHUNK:]


def mix(place, own, sources, tiles):
    return pl.pallas_call(
        mixed_kernel,
        grid_spec=pltpu.PrefetchScalarGridSpec(
            num_scalar_prefetch=1,
            grid=(BLK,),
            in_specs=[pl.BlockSpec((1, C, W), lambda i, s: (i, 0, 0))]
            + [ANY] * len(sources)
            + [pl.BlockSpec((1, FAN, W, W), lambda i, s: (i, 0, 0, 0))],
            out_specs=pl.BlockSpec((2, C, CHUNK), lambda i, s: (i, 0, 0)),
            scratch_shapes=[pltpu.VMEM((HELD, C, W), f32), pltpu.SemaphoreType.DMA((len(sources),))],
        ),
        out_shape=jax.ShapeDtypeStruct((16, C, CHUNK), f32),
        compiler_params=PARAMS,
        cost_estimate=pl.CostEstimate(flops=2 * 64 * W * W * 2 * C, bytes_accessed=13 << 20, transcendentals=0),
    )(place, own, *sources, tiles)


def weight_kernel(in_ref, thi_ref, tlo_ref, hi_ref, lo_ref):
    value = in_ref[...]
    thi_ref[...], tlo_ref[...] = split(value)
    hi_ref[...], lo_ref[...] = split(value.T)


def weight_parts(transposed):
    step = 256
    by_row = pl.BlockSpec((step, F), lambda i: (i, 0))
    by_col = pl.BlockSpec((F, step), lambda i: (0, i))
    return pl.pallas_call(
        weight_kernel,
        grid=(F // step,),
        in_specs=[by_row],
        out_specs=[by_row, by_row, by_col, by_col],
        out_shape=[jax.ShapeDtypeStruct((F, F), bf16)] * 4,
        compiler_params=PARAMS,
        cost_estimate=pl.CostEstimate(flops=F * F * 8, bytes_accessed=12 << 20, transcendentals=0),
    )(transposed)


def dense_kernel(thi_ref, tlo_ref, hi_ref, lo_ref, mixed_ref, cot_ref, hidden_ref, slope_ref, back_ref, parts):
    step = pl.program_id(0)

    @pl.when(step == 0)
    def _():
        hi, lo = split(mixed_ref[...])
        parts[:, :CHUNK] = hi
        parts[:, CHUNK:] = lo

    both = jnp.dot(thi_ref[...], parts[...], preferred_element_type=f32)
    low = jnp.dot(tlo_ref[...], parts[:, :CHUNK], preferred_element_type=f32)
    pre = both[:, :CHUNK] + (both[:, CHUNK:] + low)
    sig = jax.nn.sigmoid(pre)
    hidden_ref[...] = pre * sig
    slope = cot_ref[...] * sig * (1.0 + pre * (1.0 - sig))
    slope_ref[...] = slope
    shi, slo = split(slope)
    both = jnp.dot(hi_ref[...], jnp.concatenate([shi, slo], axis=1), preferred_element_type=f32)
    low = jnp.dot(lo_ref[...], shi, preferred_element_type=f32)
    part = both[:, :CHUNK] + (both[:, CHUNK:] + low)

    @pl.when(step == 0)
    def _():
        back_ref[...] = part

    @pl.when(step > 0)
    def _():
        back_ref[...] += part


def dense(weights, mixed, cot):
    step = 256
    by_row = pl.BlockSpec((step, F), lambda i: (i, 0))
    by_col = pl.BlockSpec((F, step), lambda i: (0, i))
    rows = pl.BlockSpec((step, CHUNK), lambda i: (i, 0))
    whole = pl.BlockSpec((F, CHUNK), lambda i: (0, 0))
    return pl.pallas_call(
        dense_kernel,
        grid=(F // step,),
        in_specs=[by_row, by_row, by_col, by_col, whole, rows],
        out_specs=[rows, rows, whole],
        out_shape=[jax.ShapeDtypeStruct((F, CHUNK), f32)] * 3,
        scratch_shapes=[pltpu.VMEM((F, 2 * CHUNK), bf16)],
        compiler_params=PARAMS,
        cost_estimate=pl.CostEstimate(flops=12 * F * F * CHUNK, bytes_accessed=10 << 20, transcendentals=F * CHUNK),
    )(*weights, mixed, cot)


def push_kernel(place_ref, back_ref, tiles_ref, diag_ref, *refs):
    outs, held, sems = refs[:13], *refs[13:]
    i = pl.program_id(0)

    @pl.when(i == 0)
    def _():
        held[...] = jnp.zeros_like(held)

    block = jnp.concatenate([back_ref[0], back_ref[1]], axis=1)
    both = jnp.concatenate(split(block), axis=0)
    for k in range(FAN):
        part = jnp.dot(both, tiles_ref[0, k], preferred_element_type=f32)
        value = part[:C] + part[C:]
        if k == 0:
            diag_ref[0] = value
        else:
            held[place_ref[i * (FAN - 1) + k - 1]] += value

    @pl.when(i == BLK - 1)
    def _():
        copies = [pltpu.make_async_copy(held.at[rows], ref, sems.at[n]) for n, (rows, ref) in enumerate(places(outs))]
        for copy in copies:
            copy.start()
        for copy in copies:
            copy.wait()


def push(place, back, tiles):
    sizes = (4, 4, 8, 8, 4, 4, 4, 8, 8, 8, 4, 4, 4)
    return pl.pallas_call(
        push_kernel,
        grid_spec=pltpu.PrefetchScalarGridSpec(
            num_scalar_prefetch=1,
            grid=(BLK,),
            in_specs=[
                pl.BlockSpec((2, C, CHUNK), lambda i, s: (i, 0, 0)),
                pl.BlockSpec((1, FAN, W, W), lambda i, s: (i, 0, 0, 0)),
            ],
            out_specs=[pl.BlockSpec((1, C, W), lambda i, s: (i, 0, 0))] + [ANY] * len(sizes),
            scratch_shapes=[pltpu.VMEM((HELD, C, W), f32), pltpu.SemaphoreType.DMA((len(sizes),))],
        ),
        out_shape=[jax.ShapeDtypeStruct((n, C, W), f32) for n in (BLK,) + sizes],
        compiler_params=PARAMS,
        cost_estimate=pl.CostEstimate(flops=2 * 64 * W * W * 2 * C, bytes_accessed=13 << 20, transcendentals=0),
    )(place, back, tiles)


def add_slots(index_ref, got, group, out_ref):
    per = got[0].shape[0]
    for s in range(3):
        for t in range(SLOTS):
            slot = group * SLOTS + t
            index = index_ref[s * per + slot]

            @pl.when(index > 0)
            def _():
                out_ref[index - 1] += got[s][slot]


def far_kernel(index_ref, a_ref, b_ref, c_ref, lo_ref, hi_ref, out_lo, out_hi, total):
    total[: BLK // 2] = lo_ref[...]
    total[BLK // 2 :] = hi_ref[...]
    add_slots(index_ref, (a_ref, b_ref, c_ref), 0, total)
    out_lo[...] = total[: BLK // 2]
    out_hi[...] = total[BLK // 2 :]


def mid_kernel(index_ref, a_ref, b_ref, c_ref, up_ref, down_ref, below_ref, above_ref, out_up, out_down):
    half = BLK // 2
    out_up[:half] = up_ref[:half] + below_ref[...]
    out_up[half:] = up_ref[half:]
    out_down[:half] = down_ref[:half]
    out_down[half:] = down_ref[half:] + above_ref[...]
    add_slots(index_ref, (a_ref, b_ref, c_ref), 0, out_up)
    add_slots(index_ref, (a_ref, b_ref, c_ref), 1, out_down)


def near_kernel(index_ref, a_ref, b_ref, c_ref, diag_ref, out):
    out[...] = diag_ref[...]
    add_slots(index_ref, (a_ref, b_ref, c_ref), 0, out)


def gather_sum(kernel, shapes, scratch, index, *args):
    return pl.pallas_call(
        kernel,
        out_shape=[jax.ShapeDtypeStruct((n, C, W), f32) for n in shapes],
        in_specs=[SMEM] + [VMEM] * len(args),
        out_specs=[VMEM] * len(shapes),
        scratch_shapes=scratch,
        compiler_params=PARAMS,
        cost_estimate=pl.CostEstimate(flops=12 * C * W, bytes_accessed=3 << 20, transcendentals=0),
    )(index, *args)


def shift(value, axis, size, by):
    return lax.ppermute(value, axis, [(i, (i + by) % size) for i in range(size)])


def over_x(pieces, sign):
    return [shift(piece, "x", NX, sign * (s + 1)) for s, piece in enumerate(pieces)]


def over_col(value):
    return lax.all_to_all(value, COL, 0, 0, tiled=True)


def on_device(features, neighbours, tiles, weight, cotangent):
    near_at, mid_at, far_at, place = tables(neighbours)
    own = features.T.reshape(C, BLK, W).transpose(1, 0, 2)

    up = shift(own, "zh", NZ, -1)
    down = shift(own, "zh", NZ, 1)
    near = over_x(pick(near_at, own), 1)
    weights = weight_parts(lax.all_gather(weight.T, COL, axis=0, tiled=True))
    cot = over_col(cotangent.T.reshape(C, 16, CHUNK).transpose(1, 0, 2)).reshape(F, CHUNK)
    far_lo = shift(up[: BLK // 2], "zh", NZ, -1)
    far_hi = shift(down[BLK // 2 :], "zh", NZ, 1)
    mid = over_x(pick(mid_at, up, down), 1)
    far = over_x(pick(far_at, far_lo, far_hi, halves=True), 1)
    own, weights, cot = lax.optimization_barrier((own, weights, cot))
    mixed = mix(place, own, [far_lo, far_hi, up, down, *near, *mid, *far], tiles)

    mixed = over_col(mixed).reshape(F, CHUNK)
    hidden, slope, back = dense(weights, mixed, cot)
    back = over_col(back.reshape(16, C, CHUNK))

    diag, lo, hi, up, down, *pieces = push(place, back, tiles)
    diag, hidden, slope, mixed = lax.optimization_barrier((diag, hidden, slope, mixed))
    near, mid, far = pieces[:3], pieces[3:6], pieces[6:]
    far = over_x(far, -1)
    far, mid = lax.optimization_barrier((far, mid))
    mid = over_x(mid, -1)
    lo, hi = gather_sum(far_kernel, (4, 4), [pltpu.VMEM((BLK, C, W), f32)], far_at, *far, lo, hi)
    below = shift(lo, "zh", NZ, 1)
    above = shift(hi, "zh", NZ, -1)
    mid, near = lax.optimization_barrier((mid, near))
    near = over_x(near, -1)
    up, down = gather_sum(mid_kernel, (8, 8), [], mid_at, *mid, up, down, below, above)
    up = shift(up, "zh", NZ, 1)
    down = shift(down, "zh", NZ, -1)
    (near,) = gather_sum(near_kernel, (8,), [], near_at, *near, diag)
    grad_features = (near + up + down).transpose(1, 0, 2).reshape(C, BLK * W).T
    hidden = over_col(hidden.reshape(16, C, CHUNK)).transpose(1, 0, 2).reshape(C, 16 * CHUNK).T

    me_c, me_l = lax.axis_index("c"), lax.axis_index("zl")
    by_core = slope.reshape(8, 2, C, CHUNK)

    def partial(core):
        rows = lax.dynamic_index_in_dim(by_core, core, 1, keepdims=False).reshape(8 * C, CHUNK)
        return lax.dot_general(
            rows, mixed, (((1,), (1,)), ((), ())), precision=lax.Precision.HIGH, preferred_element_type=f32
        )

    grad = partial(me_c) + shift(partial(1 - me_c), "c", 2, 1)
    grad = lax.all_to_all(grad.reshape(NY, 2 * C, F), "y", 0, 0, tiled=True).sum(axis=0).reshape(2, C, F)
    other = shift(lax.dynamic_index_in_dim(grad, 1 - me_l, 0, keepdims=False), "zl", 2, 1)
    grad = lax.dynamic_index_in_dim(grad, me_l, 0, keepdims=False) + other
    grad = grad.reshape(2, C // 2, 16, C).transpose(2, 1, 0, 3).reshape(16, C // 2, 2 * C)
    grad = lax.all_to_all(grad, DOM, 0, 0, tiled=True).sum(axis=0)
    grad_weight = grad.reshape(C // 2, 2, C).transpose(1, 0, 2).reshape(C, C).T
    return hidden, grad_features, grad_weight


def solution(mesh):
    fine = Mesh(mesh.devices.reshape(4, 4, 4, 2, 2), DOM + COL)
    in_specs = (P(DOM, COL), P(), P(DOM, None, None, None), P(None, COL), P(DOM, COL))
    out_specs = (P(DOM, COL), P(DOM, COL), P(DOM, COL))
    return jax.shard_map(on_device, mesh=fine, in_specs=in_specs, out_specs=out_specs, check_vma=False)
```

```python
import functools

import jax
import jax.numpy as jnp
from jax import lax
from jax.experimental import pallas as pl
from jax.experimental.pallas import tpu as pltpu
from jax.sharding import Mesh
from jax.sharding import PartitionSpec as P

DOM = ("x", "zh")
COL = ("y", "zl", "c")
NX, NZ, NY = 4, 4, 4
BLK, FAN, W, C = 8, 8, 256, 64
REFS = BLK * (FAN - 1)
SLOTS = 4
FAR = 60
HELD = FAR + 1
F = 1024
CHUNK = 128
f32, bf16 = jnp.float32, jnp.bfloat16
VMEM = pl.BlockSpec(memory_space=pltpu.VMEM)
SMEM = pl.BlockSpec(memory_space=pltpu.SMEM)
ANY = pl.BlockSpec(memory_space=pl.ANY)
PARAMS = pltpu.CompilerParams(vmem_limit_bytes=58 * 2**20)


def split(value):
    hi = value.astype(bf16)
    lo = (value - hi.astype(f32)).astype(bf16)
    return hi, lo


def tables(neighbours):
    me_x, me_z = lax.axis_index("x"), lax.axis_index("zh")
    rows = neighbours.reshape(NX, NZ, REFS)
    rows = lax.dynamic_index_in_dim(rows, me_z, 1, keepdims=False)
    rows = lax.dynamic_slice_in_dim(jnp.concatenate([rows, rows], axis=0), me_x, NX, 0)
    owner, block = rows >> 3, rows & 7
    ref = jnp.arange(REFS)
    same = (owner[:, :, None] == owner[:, None, :]) & (ref[None, :, None] > ref[None, None, :])
    rank = jnp.sum(same.astype(jnp.int32), axis=2)
    wanted = me_x * NZ + ((me_z + jnp.arange(NZ)) & (NZ - 1))
    match = (owner[None, 1:, None, :] == wanted[:, None, None, None]) & (
        rank[None, 1:, None, :] == jnp.arange(SLOTS)[None, None, :, None]
    )
    table = jnp.sum(jnp.where(match, block[None, 1:, None, :] + 1, 0), axis=3)
    e, s = ((owner[0] & 3) - me_z) & 3, (me_x - (owner[0] >> 2)) & 3
    local = jnp.where(e == 2, 0, jnp.where(e == 1, 8, 16)) + block[0]
    start = jnp.where(e == 0, 24, jnp.where(e == 2, 60, 36 + (e >> 1) * 4))
    stride = jnp.where((e & 1) == 1, 8, 4)
    place = jnp.where(s == 0, local, start + (s - 1) * stride + rank[0])
    near = table[0].reshape(12)
    mid = jnp.stack([table[1], table[3]], axis=1).reshape(24)
    far = table[2].reshape(12)
    source = ((me_x - jnp.arange(1, NX)) & 3) * NZ + ((me_z + 2) & 3)
    match = (owner[0][None, None, :] == source[:, None, None]) & (
        rank[0][None, None, :] == jnp.arange(SLOTS)[None, :, None]
    )
    far_refs = jnp.sum(jnp.where(match, ref[None, None, :] + 1, 0), axis=2).reshape(12)
    return near, mid, far, far_refs, jnp.clip(place, 0, FAR)


def pick_slots(index_ref, sources, outs):
    per = outs[0].shape[0]
    for s in range(3):
        for slot in range(per):
            index = jnp.maximum(index_ref[s * per + slot] - 1, 0)
            outs[s][slot] = sources[slot // SLOTS][index]


def pick_near_kernel(index_ref, own_ref, *outs):
    pick_slots(index_ref, (own_ref,), outs)


def pick_mid_kernel(index_ref, up_ref, down_ref, lo_ref, hi_ref, *outs):
    lo_ref[...] = up_ref[: BLK // 2]
    hi_ref[...] = down_ref[BLK // 2 :]
    pick_slots(index_ref, (up_ref, down_ref), outs)


def pick_far_kernel(index_ref, lo_ref, hi_ref, *refs):
    outs, held = refs[:3], refs[3]
    held[: BLK // 2] = lo_ref[...]
    held[BLK // 2 :] = hi_ref[...]
    pick_slots(index_ref, (held,), outs)


def pick(kernel, shapes, scratch, index, *sources):
    return pl.pallas_call(
        kernel,
        out_shape=[jax.ShapeDtypeStruct((n, C, W), f32) for n in shapes],
        in_specs=[SMEM] + [VMEM] * len(sources),
        out_specs=[VMEM] * len(shapes),
        scratch_shapes=scratch,
        compiler_params=PARAMS,
        cost_estimate=pl.CostEstimate(flops=0, bytes_accessed=2 << 20, transcendentals=0),
    )(index, *sources)


def places(refs):
    start, pairs = 0, []
    for ref in refs:
        pairs.append((pl.ds(start, ref.shape[0]), ref))
        start += ref.shape[0]
    return pairs


def mixed_kernel(place_ref, own_ref, *refs):
    sources, tiles_ref, out_ref, held, sems = refs[:10], *refs[10:]
    i = pl.program_id(0)

    @pl.when(i == 0)
    def _():
        copies = [
            pltpu.make_async_copy(ref, held.at[rows], sems.at[n]) for n, (rows, ref) in enumerate(places(sources))
        ]
        for copy in copies:
            copy.start()
        held[FAR] = jnp.zeros((C, W), f32)
        for copy in copies:
            copy.wait()

    acc = None
    for k in range(FAN):
        block = own_ref[0] if k == 0 else held[place_ref[i * (FAN - 1) + k - 1]]
        part = lax.dot_general(
            jnp.concatenate(split(block), axis=0),
            tiles_ref[0, k],
            (((1,), (1,)), ((), ())),
            preferred_element_type=f32,
        )
        acc = part if acc is None else acc + part
    out_ref[0] = acc[:C] + acc[C:]


def mix(place, own, sources, tiles):
    return pl.pallas_call(
        mixed_kernel,
        grid_spec=pltpu.PrefetchScalarGridSpec(
            num_scalar_prefetch=1,
            grid=(BLK,),
            in_specs=[pl.BlockSpec((1, C, W), lambda i, s: (i, 0, 0))]
            + [ANY] * len(sources)
            + [pl.BlockSpec((1, FAN, W, W), lambda i, s: (i, 0, 0, 0))],
            out_specs=pl.BlockSpec((1, C, W), lambda i, s: (i, 0, 0)),
            scratch_shapes=[pltpu.VMEM((HELD, C, W), f32), pltpu.SemaphoreType.DMA((len(sources),))],
        ),
        out_shape=jax.ShapeDtypeStruct((BLK, C, W), f32),
        compiler_params=PARAMS,
        cost_estimate=pl.CostEstimate(flops=2 * 64 * W * W * 2 * C, bytes_accessed=13 << 20, transcendentals=0),
    )(place, own, *sources, tiles)


def tile_copies(refs_ref, tiles_ref, held, sems):
    copies = []
    for slot in range(12):
        ref = jnp.maximum(refs_ref[slot] - 1, 0)
        i = ref // (FAN - 1)
        copies.append(
            pltpu.make_async_copy(tiles_ref.at[i, ref - i * (FAN - 1) + 1], held.at[slot], sems.at[slot])
        )
    for copy in copies:
        copy.start()
    return copies


def mix_far_kernel(refs_ref, part_ref, a_ref, b_ref, c_ref, tiles_ref, out_ref, held, total, sems):
    copies = tile_copies(refs_ref, tiles_ref, held, sems)
    total[...] = part_ref[...]
    for copy in copies:
        copy.wait()
    for slot in range(12):
        both = jnp.concatenate(split((a_ref, b_ref, c_ref)[slot // SLOTS][slot % SLOTS]), axis=0)
        part = lax.dot_general(both, held[slot], (((1,), (1,)), ((), ())), preferred_element_type=f32)
        ref = refs_ref[slot]
        total[jnp.maximum(ref - 1, 0) // (FAN - 1)] += jnp.where(ref > 0, part[:C] + part[C:], 0.0)

    for i in range(BLK):
        out_ref[2 * i] = total[i, :, :CHUNK]
        out_ref[2 * i + 1] = total[i, :, CHUNK:]


def mix_far(far_refs, part, far, tiles):
    return pl.pallas_call(
        mix_far_kernel,
        out_shape=jax.ShapeDtypeStruct((16, C, CHUNK), f32),
        in_specs=[SMEM] + [VMEM] * 4 + [ANY],
        out_specs=VMEM,
        scratch_shapes=[
            pltpu.VMEM((12, W, W), bf16),
            pltpu.VMEM((BLK, C, W), f32),
            pltpu.SemaphoreType.DMA((12,)),
        ],
        compiler_params=PARAMS,
        cost_estimate=pl.CostEstimate(flops=2 * 12 * W * W * 2 * C, bytes_accessed=4 << 20, transcendentals=0),
    )(far_refs, part, *far, tiles)


def weight_kernel(in_ref, thi_ref, tlo_ref, hi_ref, lo_ref):
    value = in_ref[...]
    thi_ref[...], tlo_ref[...] = split(value)
    hi_ref[...], lo_ref[...] = split(value.T)


def weight_parts(transposed):
    step = 256
    by_row = pl.BlockSpec((step, F), lambda i: (i, 0))
    by_col = pl.BlockSpec((F, step), lambda i: (0, i))
    return pl.pallas_call(
        weight_kernel,
        grid=(F // step,),
        in_specs=[by_row],
        out_specs=[by_row, by_row, by_col, by_col],
        out_shape=[jax.ShapeDtypeStruct((F, F), bf16)] * 4,
        compiler_params=PARAMS,
        cost_estimate=pl.CostEstimate(flops=F * F * 8, bytes_accessed=12 << 20, transcendentals=0),
    )(transposed)


def dense_kernel(thi_ref, tlo_ref, hi_ref, lo_ref, mixed_ref, cot_ref, slope_ref, out_ref, parts):
    step = pl.program_id(0)

    @pl.when(step == 0)
    def _():
        hi, lo = split(mixed_ref[...])
        parts[:, :CHUNK] = hi
        parts[:, CHUNK:] = lo

    both = jnp.dot(thi_ref[...], parts[...], preferred_element_type=f32)
    low = jnp.dot(tlo_ref[...], parts[:, :CHUNK], preferred_element_type=f32)
    pre = both[:, :CHUNK] + (both[:, CHUNK:] + low)
    sig = jax.nn.sigmoid(pre)
    hidden = (pre * sig).reshape(-1, C, CHUNK)
    out_ref[pl.ds(step * hidden.shape[0], hidden.shape[0]), C:] = hidden
    slope = cot_ref[...] * sig * (1.0 + pre * (1.0 - sig))
    slope_ref[...] = slope
    shi, slo = split(slope)
    both = jnp.dot(hi_ref[...], jnp.concatenate([shi, slo], axis=1), preferred_element_type=f32)
    low = jnp.dot(lo_ref[...], shi, preferred_element_type=f32)
    part = (both[:, :CHUNK] + (both[:, CHUNK:] + low)).reshape(16, C, CHUNK)

    @pl.when(step == 0)
    def _():
        out_ref[:, :C] = part

    @pl.when(step > 0)
    def _():
        out_ref[:, :C] += part


def dense(weights, mixed, cot):
    step = 256
    by_row = pl.BlockSpec((step, F), lambda i: (i, 0))
    by_col = pl.BlockSpec((F, step), lambda i: (0, i))
    rows = pl.BlockSpec((step, CHUNK), lambda i: (i, 0))
    whole = pl.BlockSpec((F, CHUNK), lambda i: (0, 0))
    return pl.pallas_call(
        dense_kernel,
        grid=(F // step,),
        in_specs=[by_row, by_row, by_col, by_col, whole, rows],
        out_specs=[rows, pl.BlockSpec((16, 2 * C, CHUNK), lambda i: (0, 0, 0))],
        out_shape=[jax.ShapeDtypeStruct((F, CHUNK), f32), jax.ShapeDtypeStruct((16, 2 * C, CHUNK), f32)],
        scratch_shapes=[pltpu.VMEM((F, 2 * CHUNK), bf16)],
        compiler_params=PARAMS,
        cost_estimate=pl.CostEstimate(flops=12 * F * F * CHUNK, bytes_accessed=10 << 20, transcendentals=F * CHUNK),
    )(*weights, mixed, cot)


def push_far_kernel(refs_ref, back_ref, tiles_ref, a_ref, b_ref, c_ref, held, sems):
    copies = tile_copies(refs_ref, tiles_ref, held, sems)
    for copy in copies:
        copy.wait()
    for slot in range(12):
        ref = refs_ref[slot]
        i = jnp.maximum(ref - 1, 0) // (FAN - 1)
        block = jnp.concatenate([back_ref[2 * i, :C], back_ref[2 * i + 1, :C]], axis=1)
        both = jnp.concatenate(split(block), axis=0)
        part = jnp.dot(both, held[slot], preferred_element_type=f32)
        (a_ref, b_ref, c_ref)[slot // SLOTS][slot % SLOTS] = part[:C] + part[C:]


def push_far(far_refs, back, tiles):
    return pl.pallas_call(
        push_far_kernel,
        out_shape=[jax.ShapeDtypeStruct((SLOTS, C, W), f32)] * 3,
        in_specs=[SMEM, VMEM, ANY],
        out_specs=[VMEM] * 3,
        scratch_shapes=[pltpu.VMEM((12, W, W), bf16), pltpu.SemaphoreType.DMA((12,))],
        compiler_params=PARAMS,
        cost_estimate=pl.CostEstimate(flops=2 * 12 * W * W * 2 * C, bytes_accessed=4 << 20, transcendentals=0),
    )(far_refs, back, tiles)


def push_kernel(place_ref, back_ref, tiles_ref, diag_ref, *refs):
    outs, held, sems = refs[:10], *refs[10:]
    i = pl.program_id(0)

    @pl.when(i == 0)
    def _():
        held[...] = jnp.zeros_like(held)

    block = jnp.concatenate([back_ref[0], back_ref[1]], axis=1)
    both = jnp.concatenate(split(block), axis=0)
    for k in range(FAN):
        part = jnp.dot(both, tiles_ref[0, k], preferred_element_type=f32)
        value = part[:C] + part[C:]
        if k == 0:
            diag_ref[0] = value
        else:
            held[place_ref[i * (FAN - 1) + k - 1]] += value

    @pl.when(i == BLK - 1)
    def _():
        copies = [pltpu.make_async_copy(held.at[rows], ref, sems.at[n]) for n, (rows, ref) in enumerate(places(outs))]
        for copy in copies:
            copy.start()
        for copy in copies:
            copy.wait()


def push(place, back, tiles):
    sizes = (4, 4, 8, 8, 4, 4, 4, 8, 8, 8)
    return pl.pallas_call(
        push_kernel,
        grid_spec=pltpu.PrefetchScalarGridSpec(
            num_scalar_prefetch=1,
            grid=(BLK,),
            in_specs=[
                pl.BlockSpec((2, C, CHUNK), lambda i, s: (i, 0, 0)),
                pl.BlockSpec((1, FAN, W, W), lambda i, s: (i, 0, 0, 0)),
            ],
            out_specs=[pl.BlockSpec((1, C, W), lambda i, s: (i, 0, 0))] + [ANY] * len(sizes),
            scratch_shapes=[pltpu.VMEM((HELD, C, W), f32), pltpu.SemaphoreType.DMA((len(sizes),))],
        ),
        out_shape=[jax.ShapeDtypeStruct((n, C, W), f32) for n in (BLK,) + sizes],
        compiler_params=PARAMS,
        cost_estimate=pl.CostEstimate(flops=2 * 64 * W * W * 2 * C, bytes_accessed=13 << 20, transcendentals=0),
    )(place, back, tiles)


def add_slots(index_ref, got, group, out_ref):
    per = got[0].shape[0]
    for s in range(3):
        for t in range(SLOTS):
            slot = group * SLOTS + t
            index = index_ref[s * per + slot]
            out_ref[jnp.maximum(index - 1, 0)] += jnp.where(index > 0, got[s][slot], 0.0)


def far_kernel(index_ref, a_ref, b_ref, c_ref, lo_ref, hi_ref, out_lo, out_hi, total):
    total[: BLK // 2] = lo_ref[...]
    total[BLK // 2 :] = hi_ref[...]
    add_slots(index_ref, (a_ref, b_ref, c_ref), 0, total)
    out_lo[...] = total[: BLK // 2]
    out_hi[...] = total[BLK // 2 :]


def mid_kernel(index_ref, a_ref, b_ref, c_ref, up_ref, down_ref, below_ref, above_ref, out_up, out_down):
    half = BLK // 2
    out_up[:half] = up_ref[:half] + below_ref[...]
    out_up[half:] = up_ref[half:]
    out_down[:half] = down_ref[:half]
    out_down[half:] = down_ref[half:] + above_ref[...]
    add_slots(index_ref, (a_ref, b_ref, c_ref), 0, out_up)
    add_slots(index_ref, (a_ref, b_ref, c_ref), 1, out_down)


def near_kernel(index_ref, a_ref, b_ref, c_ref, diag_ref, out):
    out[...] = diag_ref[...]
    add_slots(index_ref, (a_ref, b_ref, c_ref), 0, out)


def gather_sum(kernel, shapes, scratch, index, *args):
    return pl.pallas_call(
        kernel,
        out_shape=[jax.ShapeDtypeStruct((n, C, W), f32) for n in shapes],
        in_specs=[SMEM] + [VMEM] * len(args),
        out_specs=[VMEM] * len(shapes),
        scratch_shapes=scratch,
        compiler_params=PARAMS,
        cost_estimate=pl.CostEstimate(flops=12 * C * W, bytes_accessed=3 << 20, transcendentals=0),
    )(index, *args)


def shift(value, axis, size, by):
    return lax.ppermute(value, axis, [(i, (i + by) % size) for i in range(size)])


def over_x(pieces, sign):
    return [shift(piece, "x", NX, sign * (s + 1)) for s, piece in enumerate(pieces)]


def over_col(value):
    return lax.all_to_all(value, COL, 0, 0, tiled=True)


def grad_kernel(core_ref, slope_ref, other_ref, mixed_ref, far_ref, out_ref, wide):
    @pl.when(pl.program_id(0) == 0)
    def _():
        for n, ref in enumerate((mixed_ref, far_ref)):
            hi, lo = split(ref[...])
            for m, value in enumerate((hi, lo, hi)):
                start = (2 * m + n) * CHUNK
                wide[:, start : start + CHUNK] = value

    rows = out_ref.shape[0]
    mine, other = split(slope_ref[...].reshape(rows, CHUNK)), split(other_ref[...])
    left = jnp.concatenate([mine[0], other[0], mine[0], other[0], mine[1], other[1]], axis=1)
    out_ref[...] = lax.dot_general(left, wide[...], (((1,), (1,)), ((), ())), preferred_element_type=f32)


def grad_part(core, slope, other, mixed, mixed_other):
    steps = 4
    rows = 8 * C // steps
    whole = pl.BlockSpec((F, CHUNK), lambda i, s: (0, 0))
    return pl.pallas_call(
        grad_kernel,
        grid_spec=pltpu.PrefetchScalarGridSpec(
            num_scalar_prefetch=1,
            grid=(steps,),
            in_specs=[
                pl.BlockSpec((8 // steps, 1, C, CHUNK), lambda i, s: (i, s[0], 0, 0)),
                pl.BlockSpec((rows, CHUNK), lambda i, s: (i, 0)),
                whole,
                whole,
            ],
            out_specs=pl.BlockSpec((rows, F), lambda i, s: (i, 0)),
            scratch_shapes=[pltpu.VMEM((F, 6 * CHUNK), bf16)],
        ),
        out_shape=jax.ShapeDtypeStruct((8 * C, F), f32),
        compiler_params=PARAMS,
        cost_estimate=pl.CostEstimate(flops=6 * F * F * CHUNK, bytes_accessed=4 << 20, transcendentals=0),
    )(core.reshape(1).astype(jnp.int32), slope.reshape(8, 2, C, CHUNK), other, mixed, mixed_other)


def after(values, others):
    flat, tree = jax.tree.flatten((values, others))
    return jax.tree.unflatten(tree, lax.optimization_barrier(flat))


def on_device(features, neighbours, tiles, weight, cotangent):
    near_at, mid_at, far_at, far_refs, place = tables(neighbours)
    own = features.T.reshape(C, BLK, W).transpose(1, 0, 2)
    me_c = lax.axis_index("c")

    up = shift(own, "zh", NZ, -1)
    down = shift(own, "zh", NZ, 1)
    near = over_x(pick(pick_near_kernel, (4,) * 3, [], near_at, own), 1)
    (up, down), (near, weight_t) = after((up, down), (near, weight.T))
    weight_t = lax.all_gather(weight_t, COL, axis=0, tiled=True)
    lo, hi, *mid = pick(pick_mid_kernel, (4, 4) + (8,) * 3, [], mid_at, up, down)
    mid, cot = after(mid, cotangent.T)
    lo = shift(lo, "zh", NZ, -1)
    hi = shift(hi, "zh", NZ, 1)
    mid = over_x(mid, 1)
    cot = over_col(cot.reshape(C, 16, CHUNK).transpose(1, 0, 2)).reshape(F, CHUNK)
    (lo, hi, mid), cot = after((lo, hi, mid), cot)
    far = pick(pick_far_kernel, (4,) * 3, [pltpu.VMEM((BLK, C, W), f32)], far_at, lo, hi)
    far = over_x(far, 1)
    part = mix(place, own, [lo, hi, up, down, *near, *mid], tiles)
    mixed = mix_far(far_refs, part, far, tiles)

    mixed, weight_t = after(mixed, weight_t)
    mixed = over_col(mixed).reshape(F, CHUNK)
    weights = weight_parts(weight_t)
    slope, back = dense(weights, mixed, cot)
    back = over_col(back)
    hidden = back[:, C:].transpose(1, 0, 2).reshape(C, 16 * CHUNK).T

    other = lax.dynamic_index_in_dim(slope.reshape(8, 2, C, CHUNK), 1 - me_c, 1, keepdims=False)
    other = shift(other.reshape(8 * C, CHUNK), "c", 2, 1)
    grad = grad_part(me_c, slope, other, mixed, shift(mixed, "c", 2, 1))
    back, grad = after(back, grad)

    far = push_far(far_refs, back, tiles)
    far, grad = after(far, grad)
    far = over_x(far, -1)
    grad = lax.all_to_all(grad.reshape(8, C, F), ("y", "zl"), 0, 0, tiled=True)
    diag, lo, hi, up, down, *pieces = push(place, back, tiles)
    near, mid = pieces[:3], pieces[3:]
    far, (mid, hidden) = after(far, (mid, hidden))
    mid = over_x(mid, -1)
    lo, hi = gather_sum(far_kernel, (4, 4), [pltpu.VMEM((BLK, C, W), f32)], far_at, *far, lo, hi)
    lo = shift(lo, "zh", NZ, 1)
    hi = shift(hi, "zh", NZ, -1)
    grad = grad.sum(axis=0)
    grad = grad.reshape(2, C // 2, 16, C).transpose(2, 1, 0, 3).reshape(16, C // 2, 2 * C)
    (mid, lo, hi), (near, grad) = after((mid, lo, hi), (near, grad))
    up, down = gather_sum(mid_kernel, (8, 8), [], mid_at, *mid, up, down, lo, hi)
    (up, down), (near, grad) = after((up, down), (near, grad))
    up = shift(up, "zh", NZ, 1)
    down = shift(down, "zh", NZ, -1)
    near = over_x(near, -1)
    grad = lax.all_to_all(grad, DOM, 0, 0, tiled=True).sum(axis=0)
    (near,) = gather_sum(near_kernel, (8,), [], near_at, *near, diag)
    grad_weight = grad.reshape(C // 2, 2, C).transpose(1, 0, 2).reshape(C, C).T
    grad_features = (near + up + down).transpose(1, 0, 2).reshape(C, BLK * W).T
    return hidden, grad_features, grad_weight


def solution(mesh):
    fine = Mesh(mesh.devices.reshape(4, 4, 4, 2, 2), DOM + COL)
    in_specs = (P(DOM, COL), P(), P(DOM, None, None, None), P(None, COL), P(DOM, COL))
    out_specs = (P(DOM, COL), P(DOM, COL), P(DOM, COL))
    return jax.shard_map(on_device, mesh=fine, in_specs=in_specs, out_specs=out_specs, check_vma=False)
```

```python
import functools

import jax
import jax.numpy as jnp
from jax import lax
from jax.experimental import pallas as pl
from jax.experimental.pallas import tpu as pltpu
from jax.sharding import Mesh
from jax.sharding import PartitionSpec as P

DOM = ("x", "zh")
COL = ("y", "zl", "c")
NX, NZ, NY = 4, 4, 4
BLK, FAN, W, C = 8, 8, 256, 64
REFS = BLK * (FAN - 1)
SLOTS = 4
FAR = 60
HELD = FAR + 1
F = 1024
CHUNK = 128
f32, bf16 = jnp.float32, jnp.bfloat16
VMEM = pl.BlockSpec(memory_space=pltpu.VMEM)
SMEM = pl.BlockSpec(memory_space=pltpu.SMEM)
ANY = pl.BlockSpec(memory_space=pl.ANY)
PARAMS = pltpu.CompilerParams(vmem_limit_bytes=58 * 2**20)
SMALL = pltpu.CompilerParams(vmem_limit_bytes=10 * 2**20)


def split(value):
    hi = value.astype(bf16)
    lo = (value - hi.astype(f32)).astype(bf16)
    return hi, lo


def tables(neighbours):
    me_x, me_z = lax.axis_index("x"), lax.axis_index("zh")
    rows = neighbours.reshape(NX, NZ, REFS)
    rows = lax.dynamic_index_in_dim(rows, me_z, 1, keepdims=False)
    rows = lax.dynamic_slice_in_dim(jnp.concatenate([rows, rows], axis=0), me_x, NX, 0)
    owner, block = rows >> 3, rows & 7
    ref = jnp.arange(REFS)
    same = (owner[:, :, None] == owner[:, None, :]) & (ref[None, :, None] > ref[None, None, :])
    rank = jnp.sum(same.astype(jnp.int32), axis=2)
    wanted = me_x * NZ + ((me_z + jnp.arange(NZ)) & (NZ - 1))
    match = (owner[None, 1:, None, :] == wanted[:, None, None, None]) & (
        rank[None, 1:, None, :] == jnp.arange(SLOTS)[None, None, :, None]
    )
    table = jnp.sum(jnp.where(match, block[None, 1:, None, :] + 1, 0), axis=3)
    e, s = ((owner[0] & 3) - me_z) & 3, (me_x - (owner[0] >> 2)) & 3
    local = jnp.where(e == 2, 0, jnp.where(e == 1, 8, 16)) + block[0]
    start = jnp.where(e == 0, 24, jnp.where(e == 2, 60, 36 + (e >> 1) * 4))
    stride = jnp.where((e & 1) == 1, 8, 4)
    place = jnp.where(s == 0, local, start + (s - 1) * stride + rank[0])
    near = table[0].reshape(12)
    mid = jnp.stack([table[1], table[3]], axis=1).reshape(24)
    far = table[2].reshape(12)
    source = ((me_x - jnp.arange(1, NX)) & 3) * NZ + ((me_z + 2) & 3)
    match = (owner[0][None, None, :] == source[:, None, None]) & (
        rank[0][None, None, :] == jnp.arange(SLOTS)[None, :, None]
    )
    far_refs = jnp.sum(jnp.where(match, ref[None, None, :] + 1, 0), axis=2).reshape(12)
    return near, mid, far, far_refs, jnp.clip(place, 0, FAR)


def pick_slots(index_ref, sources, outs):
    per = outs[0].shape[0]
    for s in range(3):
        for slot in range(per):
            index = jnp.maximum(index_ref[s * per + slot] - 1, 0)
            outs[s][slot] = sources[slot // SLOTS][index]


def pick_near_kernel(index_ref, own_ref, *outs):
    pick_slots(index_ref, (own_ref,), outs)


def pick_mid_kernel(index_ref, up_ref, down_ref, lo_ref, hi_ref, *outs):
    lo_ref[...] = up_ref[: BLK // 2]
    hi_ref[...] = down_ref[BLK // 2 :]
    pick_slots(index_ref, (up_ref, down_ref), outs)


def pick_far_kernel(index_ref, lo_ref, hi_ref, *refs):
    outs, held = refs[:3], refs[3]
    held[: BLK // 2] = lo_ref[...]
    held[BLK // 2 :] = hi_ref[...]
    pick_slots(index_ref, (held,), outs)


def pick(kernel, shapes, scratch, index, *sources):
    return pl.pallas_call(
        kernel,
        out_shape=[jax.ShapeDtypeStruct((n, C, W), f32) for n in shapes],
        in_specs=[SMEM] + [VMEM] * len(sources),
        out_specs=[VMEM] * len(shapes),
        scratch_shapes=scratch,
        compiler_params=SMALL,
        cost_estimate=pl.CostEstimate(flops=0, bytes_accessed=2 << 20, transcendentals=0),
    )(index, *sources)


def places(refs):
    start, pairs = 0, []
    for ref in refs:
        pairs.append((pl.ds(start, ref.shape[0]), ref))
        start += ref.shape[0]
    return pairs


def mixed_kernel(place_ref, own_ref, *refs):
    sources, tiles_ref, out_ref, held, sems = refs[:10], *refs[10:]
    i = pl.program_id(0)

    @pl.when(i == 0)
    def _():
        copies = [
            pltpu.make_async_copy(ref, held.at[rows], sems.at[n]) for n, (rows, ref) in enumerate(places(sources))
        ]
        for copy in copies:
            copy.start()
        held[FAR] = jnp.zeros((C, W), f32)
        for copy in copies:
            copy.wait()

    for j in range(2):
        acc = None
        for k in range(FAN):
            block = own_ref[j] if k == 0 else held[place_ref[(2 * i + j) * (FAN - 1) + k - 1]]
            part = lax.dot_general(
                jnp.concatenate(split(block), axis=0),
                tiles_ref[j, k],
                (((1,), (1,)), ((), ())),
                preferred_element_type=f32,
            )
            acc = part if acc is None else acc + part
        out_ref[j] = acc[:C] + acc[C:]


def mix(place, own, sources, tiles):
    return pl.pallas_call(
        mixed_kernel,
        grid_spec=pltpu.PrefetchScalarGridSpec(
            num_scalar_prefetch=1,
            grid=(BLK // 2,),
            in_specs=[pl.BlockSpec((2, C, W), lambda i, s: (i, 0, 0))]
            + [ANY] * len(sources)
            + [pl.BlockSpec((2, FAN, W, W), lambda i, s: (i, 0, 0, 0))],
            out_specs=pl.BlockSpec((2, C, W), lambda i, s: (i, 0, 0)),
            scratch_shapes=[pltpu.VMEM((HELD, C, W), f32), pltpu.SemaphoreType.DMA((len(sources),))],
        ),
        out_shape=jax.ShapeDtypeStruct((BLK, C, W), f32),
        compiler_params=PARAMS,
        cost_estimate=pl.CostEstimate(flops=2 * 64 * W * W * 2 * C, bytes_accessed=13 << 20, transcendentals=0),
    )(place, own, *sources, tiles)


def tile_copies(refs_ref, tiles_ref, held, sems):
    copies = []
    for slot in range(12):
        ref = jnp.maximum(refs_ref[slot] - 1, 0)
        i = ref // (FAN - 1)
        copies.append(
            pltpu.make_async_copy(tiles_ref.at[i, ref - i * (FAN - 1) + 1], held.at[slot], sems.at[slot])
        )
    for copy in copies:
        copy.start()
    return copies


def mix_far_kernel(refs_ref, part_ref, a_ref, b_ref, c_ref, tiles_ref, out_ref, held, total, sems):
    copies = tile_copies(refs_ref, tiles_ref, held, sems)
    total[...] = part_ref[...]
    for copy in copies:
        copy.wait()
    for slot in range(12):
        both = jnp.concatenate(split((a_ref, b_ref, c_ref)[slot // SLOTS][slot % SLOTS]), axis=0)
        part = lax.dot_general(both, held[slot], (((1,), (1,)), ((), ())), preferred_element_type=f32)
        ref = refs_ref[slot]
        total[jnp.maximum(ref - 1, 0) // (FAN - 1)] += jnp.where(ref > 0, part[:C] + part[C:], 0.0)

    for i in range(BLK):
        out_ref[2 * i] = total[i, :, :CHUNK]
        out_ref[2 * i + 1] = total[i, :, CHUNK:]


def mix_far(far_refs, part, far, tiles):
    return pl.pallas_call(
        mix_far_kernel,
        out_shape=jax.ShapeDtypeStruct((16, C, CHUNK), f32),
        in_specs=[SMEM] + [VMEM] * 4 + [ANY],
        out_specs=VMEM,
        scratch_shapes=[
            pltpu.VMEM((12, W, W), bf16),
            pltpu.VMEM((BLK, C, W), f32),
            pltpu.SemaphoreType.DMA((12,)),
        ],
        compiler_params=PARAMS,
        cost_estimate=pl.CostEstimate(flops=2 * 12 * W * W * 2 * C, bytes_accessed=4 << 20, transcendentals=0),
    )(far_refs, part, *far, tiles)


def dense_kernel(weight_ref, mixed_ref, cot_ref, slope_ref, out_ref, held, sems):
    step = 256
    copies = []
    for j in range(F // step):
        rows = pl.ds(j * step, step)
        copies.append(pltpu.make_async_copy(weight_ref.at[rows], held.at[rows], sems.at[j]))
    for copy in copies:
        copy.start()
    mhi, mlo = split(mixed_ref[...])
    parts = jnp.concatenate([mhi, mlo], axis=1)
    back = None
    for j, copy in enumerate(copies):
        rows = pl.ds(j * step, step)
        copy.wait()
        whi, wlo = split(held[rows])
        both = jnp.dot(whi, parts, preferred_element_type=f32)
        low = jnp.dot(wlo, mhi, preferred_element_type=f32)
        pre = both[:, :CHUNK] + (both[:, CHUNK:] + low)
        sig = jax.nn.sigmoid(pre)
        out_ref[pl.ds(j * step // C, step // C), C:] = (pre * sig).reshape(step // C, C, CHUNK)
        slope = cot_ref[rows] * sig * (1.0 + pre * (1.0 - sig))
        slope_ref[rows] = slope
        shi, slo = split(slope)
        over_out = (((0,), (0,)), ((), ()))
        both = lax.dot_general(whi, jnp.concatenate([shi, slo], axis=1), over_out, preferred_element_type=f32)
        low = lax.dot_general(wlo, shi, over_out, preferred_element_type=f32)
        part = both[:, :CHUNK] + (both[:, CHUNK:] + low)
        back = part if back is None else back + part
    out_ref[:, :C] = back.reshape(16, C, CHUNK)


def dense(weight_t, mixed, cot):
    return pl.pallas_call(
        dense_kernel,
        in_specs=[ANY, VMEM, VMEM],
        out_specs=[VMEM, VMEM],
        out_shape=[jax.ShapeDtypeStruct((F, CHUNK), f32), jax.ShapeDtypeStruct((16, 2 * C, CHUNK), f32)],
        scratch_shapes=[pltpu.VMEM((F, F), f32), pltpu.SemaphoreType.DMA((4,))],
        compiler_params=PARAMS,
        cost_estimate=pl.CostEstimate(flops=12 * F * F * CHUNK, bytes_accessed=8 << 20, transcendentals=F * CHUNK),
    )(weight_t, mixed, cot)


def push_far_kernel(refs_ref, back_ref, tiles_ref, a_ref, b_ref, c_ref, held, sems):
    copies = tile_copies(refs_ref, tiles_ref, held, sems)
    for copy in copies:
        copy.wait()
    for slot in range(12):
        ref = refs_ref[slot]
        i = jnp.maximum(ref - 1, 0) // (FAN - 1)
        block = jnp.concatenate([back_ref[2 * i, :C], back_ref[2 * i + 1, :C]], axis=1)
        both = jnp.concatenate(split(block), axis=0)
        part = jnp.dot(both, held[slot], preferred_element_type=f32)
        (a_ref, b_ref, c_ref)[slot // SLOTS][slot % SLOTS] = part[:C] + part[C:]


def push_far(far_refs, back, tiles):
    return pl.pallas_call(
        push_far_kernel,
        out_shape=[jax.ShapeDtypeStruct((SLOTS, C, W), f32)] * 3,
        in_specs=[SMEM, VMEM, ANY],
        out_specs=[VMEM] * 3,
        scratch_shapes=[pltpu.VMEM((12, W, W), bf16), pltpu.SemaphoreType.DMA((12,))],
        compiler_params=PARAMS,
        cost_estimate=pl.CostEstimate(flops=2 * 12 * W * W * 2 * C, bytes_accessed=4 << 20, transcendentals=0),
    )(far_refs, back, tiles)


def push_kernel(place_ref, back_ref, tiles_ref, diag_ref, *refs):
    outs, held, tiles, out_sems, tile_sems = refs[:10], *refs[10:]
    tile_copies = [pltpu.make_async_copy(tiles_ref.at[i], tiles.at[i], tile_sems.at[i]) for i in range(BLK)]
    for copy in tile_copies:
        copy.start()
    held[...] = jnp.zeros_like(held)
    for i in range(BLK):
        block = jnp.concatenate([back_ref[2 * i, :C], back_ref[2 * i + 1, :C]], axis=1)
        both = jnp.concatenate(split(block), axis=0)
        tile_copies[i].wait()
        for k in range(FAN):
            part = jnp.dot(both, tiles[i, k], preferred_element_type=f32)
            value = part[:C] + part[C:]
            if k == 0:
                diag_ref[i] = value
            else:
                held[place_ref[i * (FAN - 1) + k - 1]] += value
    copies = [pltpu.make_async_copy(held.at[rows], ref, out_sems.at[n]) for n, (rows, ref) in enumerate(places(outs))]
    for copy in copies:
        copy.start()
    for copy in copies:
        copy.wait()


def push(place, back, tiles):
    sizes = (4, 4, 8, 8, 4, 4, 4, 8, 8, 8)
    return pl.pallas_call(
        push_kernel,
        in_specs=[SMEM, VMEM, ANY],
        out_specs=[VMEM] + [ANY] * len(sizes),
        out_shape=[jax.ShapeDtypeStruct((n, C, W), f32) for n in (BLK,) + sizes],
        scratch_shapes=[
            pltpu.VMEM((HELD, C, W), f32),
            pltpu.VMEM((BLK, FAN, W, W), bf16),
            pltpu.SemaphoreType.DMA((len(sizes),)),
            pltpu.SemaphoreType.DMA((BLK,)),
        ],
        compiler_params=PARAMS,
        cost_estimate=pl.CostEstimate(flops=2 * 64 * W * W * 2 * C, bytes_accessed=13 << 20, transcendentals=0),
    )(place, back, tiles)


def add_slots(index_ref, got, group, out_ref):
    per = got[0].shape[0]
    for s in range(3):
        for t in range(SLOTS):
            slot = group * SLOTS + t
            index = index_ref[s * per + slot]
            out_ref[jnp.maximum(index - 1, 0)] += jnp.where(index > 0, got[s][slot], 0.0)


def far_kernel(index_ref, a_ref, b_ref, c_ref, lo_ref, hi_ref, out_lo, out_hi, total):
    total[: BLK // 2] = lo_ref[...]
    total[BLK // 2 :] = hi_ref[...]
    add_slots(index_ref, (a_ref, b_ref, c_ref), 0, total)
    out_lo[...] = total[: BLK // 2]
    out_hi[...] = total[BLK // 2 :]


def mid_kernel(index_ref, a_ref, b_ref, c_ref, up_ref, down_ref, below_ref, above_ref, out_up, out_down):
    half = BLK // 2
    out_up[:half] = up_ref[:half] + below_ref[...]
    out_up[half:] = up_ref[half:]
    out_down[:half] = down_ref[:half]
    out_down[half:] = down_ref[half:] + above_ref[...]
    add_slots(index_ref, (a_ref, b_ref, c_ref), 0, out_up)
    add_slots(index_ref, (a_ref, b_ref, c_ref), 1, out_down)


def near_kernel(index_ref, a_ref, b_ref, c_ref, diag_ref, out):
    out[...] = diag_ref[...]
    add_slots(index_ref, (a_ref, b_ref, c_ref), 0, out)


def gather_sum(kernel, shapes, scratch, index, *args):
    return pl.pallas_call(
        kernel,
        out_shape=[jax.ShapeDtypeStruct((n, C, W), f32) for n in shapes],
        in_specs=[SMEM] + [VMEM] * len(args),
        out_specs=[VMEM] * len(shapes),
        scratch_shapes=scratch,
        compiler_params=SMALL,
        cost_estimate=pl.CostEstimate(flops=12 * C * W, bytes_accessed=3 << 20, transcendentals=0),
    )(index, *args)


def shift(value, axis, size, by):
    return lax.ppermute(value, axis, [(i, (i + by) % size) for i in range(size)])


def over_x(pieces, sign):
    return [shift(piece, "x", NX, sign * (s + 1)) for s, piece in enumerate(pieces)]


def over_col(value):
    return lax.all_to_all(value, COL, 0, 0, tiled=True)


def grad_kernel(core_ref, slope_ref, other_ref, mixed_ref, far_ref, out_ref, wide):
    @pl.when(pl.program_id(0) == 0)
    def _():
        for n, ref in enumerate((mixed_ref, far_ref)):
            hi, lo = split(ref[...])
            for m, value in enumerate((hi, lo, hi)):
                start = (2 * m + n) * CHUNK
                wide[:, start : start + CHUNK] = value

    rows = out_ref.shape[0]
    mine, other = split(slope_ref[...].reshape(rows, CHUNK)), split(other_ref[...])
    left = jnp.concatenate([mine[0], other[0], mine[0], other[0], mine[1], other[1]], axis=1)
    out_ref[...] = lax.dot_general(left, wide[...], (((1,), (1,)), ((), ())), preferred_element_type=f32)


def grad_part(core, slope, other, mixed, mixed_other):
    steps = 4
    rows = 8 * C // steps
    whole = pl.BlockSpec((F, CHUNK), lambda i, s: (0, 0))
    return pl.pallas_call(
        grad_kernel,
        grid_spec=pltpu.PrefetchScalarGridSpec(
            num_scalar_prefetch=1,
            grid=(steps,),
            in_specs=[
                pl.BlockSpec((8 // steps, 1, C, CHUNK), lambda i, s: (i, s[0], 0, 0)),
                pl.BlockSpec((rows, CHUNK), lambda i, s: (i, 0)),
                whole,
                whole,
            ],
            out_specs=pl.BlockSpec((rows, F), lambda i, s: (i, 0)),
            scratch_shapes=[pltpu.VMEM((F, 6 * CHUNK), bf16)],
        ),
        out_shape=jax.ShapeDtypeStruct((8 * C, F), f32),
        compiler_params=PARAMS,
        cost_estimate=pl.CostEstimate(flops=6 * F * F * CHUNK, bytes_accessed=4 << 20, transcendentals=0),
    )(core.reshape(1).astype(jnp.int32), slope.reshape(8, 2, C, CHUNK), other, mixed, mixed_other)


def after(values, others):
    flat, tree = jax.tree.flatten((values, others))
    return jax.tree.unflatten(tree, lax.optimization_barrier(flat))


def on_device(features, neighbours, tiles, weight, cotangent):
    near_at, mid_at, far_at, far_refs, place = tables(neighbours)
    own = features.T.reshape(C, BLK, W).transpose(1, 0, 2)
    me_c = lax.axis_index("c")

    up = shift(own, "zh", NZ, -1)
    down = shift(own, "zh", NZ, 1)
    near = over_x(pick(pick_near_kernel, (4,) * 3, [], near_at, own), 1)
    cot = over_col(cotangent.T.reshape(C, 16, CHUNK).transpose(1, 0, 2)).reshape(F, CHUNK)
    (up, down), (near, cot, weight_t) = after((up, down), (near, cot, weight.T))
    weight_t = lax.all_gather(weight_t, COL, axis=0, tiled=True)
    lo, hi, *mid = pick(pick_mid_kernel, (4, 4) + (8,) * 3, [], mid_at, up, down)
    lo = shift(lo, "zh", NZ, -1)
    hi = shift(hi, "zh", NZ, 1)
    mid = over_x(mid, 1)
    lo, hi, mid = lax.optimization_barrier((lo, hi, mid))
    far = pick(pick_far_kernel, (4,) * 3, [pltpu.VMEM((BLK, C, W), f32)], far_at, lo, hi)
    far = over_x(far, 1)
    part = mix(place, own, [lo, hi, up, down, *near, *mid], tiles)
    mixed = mix_far(far_refs, part, far, tiles)

    mixed = over_col(mixed).reshape(F, CHUNK)
    slope, back = dense(weight_t, mixed, cot)
    back = over_col(back)
    hidden = back[:, C:].transpose(1, 0, 2).reshape(C, 16 * CHUNK).T

    other = lax.dynamic_index_in_dim(slope.reshape(8, 2, C, CHUNK), 1 - me_c, 1, keepdims=False)
    other = shift(other.reshape(8 * C, CHUNK), "c", 2, 1)
    grad = grad_part(me_c, slope, other, mixed, shift(mixed, "c", 2, 1))
    back, grad = after(back, grad)

    far = push_far(far_refs, back, tiles)
    far = over_x(far, -1)
    grad = lax.all_to_all(grad.reshape(8, C, F), ("y", "zl"), 0, 0, tiled=True)
    diag, lo, hi, up, down, *pieces = push(place, back, tiles)
    near, mid = pieces[:3], pieces[3:]
    far, (mid, hidden) = after(far, (mid, hidden))
    mid = over_x(mid, -1)
    lo, hi = gather_sum(far_kernel, (4, 4), [pltpu.VMEM((BLK, C, W), f32)], far_at, *far, lo, hi)
    lo = shift(lo, "zh", NZ, 1)
    hi = shift(hi, "zh", NZ, -1)
    grad = grad.sum(axis=0).reshape(C, NX, W).transpose(1, 0, 2)
    (mid, lo, hi), (near, grad) = after((mid, lo, hi), (near, grad))
    up, down = gather_sum(mid_kernel, (8, 8), [], mid_at, *mid, up, down, lo, hi)
    (up, down), (near, grad) = after((up, down), (near, grad))
    up = shift(up, "zh", NZ, 1)
    down = shift(down, "zh", NZ, -1)
    near = over_x(near, -1)
    grad = lax.all_to_all(grad, "x", 0, 0, tiled=True).sum(axis=0)
    grad = grad.reshape(2, C // 2, NZ, C).transpose(2, 1, 0, 3).reshape(NZ, C // 2, 2 * C)
    grad = lax.all_to_all(grad, "zh", 0, 0, tiled=True).sum(axis=0)
    (near,) = gather_sum(near_kernel, (8,), [], near_at, *near, diag)
    grad_weight = grad.reshape(C // 2, 2, C).transpose(1, 0, 2).reshape(C, C).T
    grad_features = (near + up + down).transpose(1, 0, 2).reshape(C, BLK * W).T
    return hidden, grad_features, grad_weight


def solution(mesh):
    fine = Mesh(mesh.devices.reshape(4, 4, 4, 2, 2), DOM + COL)
    in_specs = (P(DOM, COL), P(), P(DOM, None, None, None), P(None, COL), P(DOM, COL))
    out_specs = (P(DOM, COL), P(DOM, COL), P(DOM, COL))
    return jax.shard_map(on_device, mesh=fine, in_specs=in_specs, out_specs=out_specs, check_vma=False)
```

```python
import functools

import jax
import jax.numpy as jnp
from jax import lax
from jax.experimental import pallas as pl
from jax.experimental.pallas import tpu as pltpu
from jax.sharding import Mesh
from jax.sharding import PartitionSpec as P

DOM = ("x", "zh")
COL = ("y", "zl", "c")
NX, NZ, NY = 4, 4, 4
BLK, FAN, W, C = 8, 8, 256, 64
REFS = BLK * (FAN - 1)
SLOTS = 4
FAR = 60
HELD = FAR + 1
F = 1024
CHUNK = 128
f32, bf16 = jnp.float32, jnp.bfloat16
VMEM = pl.BlockSpec(memory_space=pltpu.VMEM)
SMEM = pl.BlockSpec(memory_space=pltpu.SMEM)
ANY = pl.BlockSpec(memory_space=pl.ANY)
PARAMS = pltpu.CompilerParams(vmem_limit_bytes=58 * 2**20)
SMALL = pltpu.CompilerParams(vmem_limit_bytes=10 * 2**20)


def split(value):
    hi = value.astype(bf16)
    lo = (value - hi.astype(f32)).astype(bf16)
    return hi, lo


def tables(neighbours):
    me_x, me_z = lax.axis_index("x"), lax.axis_index("zh")
    rows = neighbours.reshape(NX, NZ, REFS)
    rows = lax.dynamic_index_in_dim(rows, me_z, 1, keepdims=False)
    rows = lax.dynamic_slice_in_dim(jnp.concatenate([rows, rows], axis=0), me_x, NX, 0)
    owner, block = rows >> 3, rows & 7
    ref = jnp.arange(REFS)
    same = (owner[:, :, None] == owner[:, None, :]) & (ref[None, :, None] > ref[None, None, :])
    rank = jnp.sum(same.astype(jnp.int32), axis=2)
    wanted = me_x * NZ + ((me_z + jnp.arange(NZ)) & (NZ - 1))
    match = (owner[None, 1:, None, :] == wanted[:, None, None, None]) & (
        rank[None, 1:, None, :] == jnp.arange(SLOTS)[None, None, :, None]
    )
    table = jnp.sum(jnp.where(match, block[None, 1:, None, :] + 1, 0), axis=3)
    e, s = ((owner[0] & 3) - me_z) & 3, (me_x - (owner[0] >> 2)) & 3
    local = jnp.where(e == 2, 0, jnp.where(e == 1, 8, 16)) + block[0]
    start = jnp.where(e == 0, 24, jnp.where(e == 2, 60, 36 + (e >> 1) * 4))
    stride = jnp.where((e & 1) == 1, 8, 4)
    place = jnp.where(s == 0, local, start + (s - 1) * stride + rank[0])
    near = table[0].reshape(12)
    mid = jnp.stack([table[1], table[3]], axis=1).reshape(24)
    far = table[2].reshape(12)
    source = ((me_x - jnp.arange(1, NX)) & 3) * NZ + ((me_z + 2) & 3)
    match = (owner[0][None, None, :] == source[:, None, None]) & (
        rank[0][None, None, :] == jnp.arange(SLOTS)[None, :, None]
    )
    far_refs = jnp.sum(jnp.where(match, ref[None, None, :] + 1, 0), axis=2).reshape(12)
    return near, mid, far, far_refs, jnp.clip(place, 0, FAR)


def pick_slots(index_ref, sources, outs):
    per = outs[0].shape[0]
    for s in range(3):
        for slot in range(per):
            index = jnp.maximum(index_ref[s * per + slot] - 1, 0)
            outs[s][slot] = sources[slot // SLOTS][index]


def pick_near_kernel(index_ref, own_ref, *outs):
    pick_slots(index_ref, (own_ref,), outs)


def pick_mid_kernel(index_ref, up_ref, down_ref, lo_ref, hi_ref, *outs):
    lo_ref[...] = up_ref[: BLK // 2]
    hi_ref[...] = down_ref[BLK // 2 :]
    pick_slots(index_ref, (up_ref, down_ref), outs)


def pick_far_kernel(index_ref, lo_ref, hi_ref, *refs):
    outs, held = refs[:3], refs[3]
    held[: BLK // 2] = lo_ref[...]
    held[BLK // 2 :] = hi_ref[...]
    pick_slots(index_ref, (held,), outs)


def pick(kernel, shapes, scratch, index, *sources):
    return pl.pallas_call(
        kernel,
        out_shape=[jax.ShapeDtypeStruct((n, C, W), f32) for n in shapes],
        in_specs=[SMEM] + [VMEM] * len(sources),
        out_specs=[VMEM] * len(shapes),
        scratch_shapes=scratch,
        compiler_params=SMALL,
        cost_estimate=pl.CostEstimate(flops=0, bytes_accessed=2 << 20, transcendentals=0),
    )(index, *sources)


def places(refs):
    start, pairs = 0, []
    for ref in refs:
        pairs.append((pl.ds(start, ref.shape[0]), ref))
        start += ref.shape[0]
    return pairs


def mixed_kernel(place_ref, own_ref, *refs):
    sources, tiles_ref, out_ref, held, sems = refs[:10], *refs[10:]
    i = pl.program_id(0)

    @pl.when(i == 0)
    def _():
        copies = [
            pltpu.make_async_copy(ref, held.at[rows], sems.at[n]) for n, (rows, ref) in enumerate(places(sources))
        ]
        for copy in copies:
            copy.start()
        held[FAR] = jnp.zeros((C, W), f32)
        for copy in copies:
            copy.wait()

    for j in range(2):
        acc = None
        for k in range(FAN):
            block = own_ref[j] if k == 0 else held[place_ref[(2 * i + j) * (FAN - 1) + k - 1]]
            part = lax.dot_general(
                jnp.concatenate(split(block), axis=0),
                tiles_ref[j, k],
                (((1,), (1,)), ((), ())),
                preferred_element_type=f32,
            )
            acc = part if acc is None else acc + part
        out_ref[j] = acc[:C] + acc[C:]


def mix(place, own, sources, tiles):
    return pl.pallas_call(
        mixed_kernel,
        grid_spec=pltpu.PrefetchScalarGridSpec(
            num_scalar_prefetch=1,
            grid=(BLK // 2,),
            in_specs=[pl.BlockSpec((2, C, W), lambda i, s: (i, 0, 0))]
            + [ANY] * len(sources)
            + [pl.BlockSpec((2, FAN, W, W), lambda i, s: (i, 0, 0, 0))],
            out_specs=pl.BlockSpec((2, C, W), lambda i, s: (i, 0, 0)),
            scratch_shapes=[pltpu.VMEM((HELD, C, W), f32), pltpu.SemaphoreType.DMA((len(sources),))],
        ),
        out_shape=jax.ShapeDtypeStruct((BLK, C, W), f32),
        compiler_params=PARAMS,
        cost_estimate=pl.CostEstimate(flops=2 * 64 * W * W * 2 * C, bytes_accessed=13 << 20, transcendentals=0),
    )(place, own, *sources, tiles)


def far_tiles_kernel(refs_ref, tiles_ref, out_ref, sems):
    copies = []
    for slot in range(12):
        ref = jnp.maximum(refs_ref[slot] - 1, 0)
        i = ref // (FAN - 1)
        copies.append(
            pltpu.make_async_copy(tiles_ref.at[i, ref - i * (FAN - 1) + 1], out_ref.at[slot], sems.at[slot])
        )
    for copy in copies:
        copy.start()
    for copy in copies:
        copy.wait()


def far_tiles(far_refs, tiles):
    return pl.pallas_call(
        far_tiles_kernel,
        out_shape=jax.ShapeDtypeStruct((12, W, W), bf16),
        in_specs=[SMEM, ANY],
        out_specs=VMEM,
        scratch_shapes=[pltpu.SemaphoreType.DMA((12,))],
        compiler_params=PARAMS,
        cost_estimate=pl.CostEstimate(flops=0, bytes_accessed=3 << 20, transcendentals=0),
    )(far_refs, tiles)


def mix_far_kernel(refs_ref, part_ref, a_ref, b_ref, c_ref, tiles_ref, out_ref, total):
    total[...] = part_ref[...]
    for slot in range(12):
        both = jnp.concatenate(split((a_ref, b_ref, c_ref)[slot // SLOTS][slot % SLOTS]), axis=0)
        part = lax.dot_general(both, tiles_ref[slot], (((1,), (1,)), ((), ())), preferred_element_type=f32)
        ref = refs_ref[slot]
        total[jnp.maximum(ref - 1, 0) // (FAN - 1)] += jnp.where(ref > 0, part[:C] + part[C:], 0.0)
    for i in range(BLK):
        out_ref[2 * i] = total[i, :, :CHUNK]
        out_ref[2 * i + 1] = total[i, :, CHUNK:]


def mix_far(far_refs, part, far, tiles):
    return pl.pallas_call(
        mix_far_kernel,
        out_shape=jax.ShapeDtypeStruct((16, C, CHUNK), f32),
        in_specs=[SMEM] + [VMEM] * 5,
        out_specs=VMEM,
        scratch_shapes=[pltpu.VMEM((BLK, C, W), f32)],
        compiler_params=SMALL,
        cost_estimate=pl.CostEstimate(flops=2 * 12 * W * W * 2 * C, bytes_accessed=4 << 20, transcendentals=0),
    )(far_refs, part, *far, tiles)


def dense_kernel(weight_ref, mixed_ref, cot_ref, slope_ref, out_ref, held, sems):
    step = F // 2
    copies = []
    for j in range(F // step):
        rows = pl.ds(j * step, step)
        copies.append(pltpu.make_async_copy(weight_ref.at[rows], held.at[rows], sems.at[j]))
    for copy in copies:
        copy.start()
    mhi, mlo = split(mixed_ref[...])
    parts = jnp.concatenate([mhi, mlo], axis=1)
    back = None
    for j, copy in enumerate(copies):
        rows = pl.ds(j * step, step)
        copy.wait()
        whi, wlo = split(held[rows])
        both = jnp.dot(whi, parts, preferred_element_type=f32)
        low = jnp.dot(wlo, mhi, preferred_element_type=f32)
        pre = both[:, :CHUNK] + (both[:, CHUNK:] + low)
        sig = jax.nn.sigmoid(pre)
        out_ref[pl.ds(j * step // C, step // C), C:] = (pre * sig).reshape(step // C, C, CHUNK)
        slope = cot_ref[rows] * sig * (1.0 + pre * (1.0 - sig))
        slope_ref[rows] = slope
        shi, slo = split(slope.T)
        both = jnp.dot(jnp.concatenate([shi, slo], axis=0), whi, preferred_element_type=f32)
        low = jnp.dot(shi, wlo, preferred_element_type=f32)
        part = both[:CHUNK] + (both[CHUNK:] + low)
        back = part if back is None else back + part
    out_ref[:, :C] = back.T.reshape(16, C, CHUNK)


def dense(weight_t, mixed, cot):
    return pl.pallas_call(
        dense_kernel,
        in_specs=[ANY, VMEM, VMEM],
        out_specs=[VMEM, VMEM],
        out_shape=[jax.ShapeDtypeStruct((F, CHUNK), f32), jax.ShapeDtypeStruct((16, 2 * C, CHUNK), f32)],
        scratch_shapes=[pltpu.VMEM((F, F), f32), pltpu.SemaphoreType.DMA((2,))],
        compiler_params=PARAMS,
        cost_estimate=pl.CostEstimate(flops=12 * F * F * CHUNK, bytes_accessed=8 << 20, transcendentals=F * CHUNK),
    )(weight_t, mixed, cot)


def push_far_kernel(refs_ref, back_ref, tiles_ref, a_ref, b_ref, c_ref):
    for slot in range(12):
        i = jnp.maximum(refs_ref[slot] - 1, 0) // (FAN - 1)
        block = jnp.concatenate([back_ref[2 * i, :C], back_ref[2 * i + 1, :C]], axis=1)
        both = jnp.concatenate(split(block), axis=0)
        part = jnp.dot(both, tiles_ref[slot], preferred_element_type=f32)
        (a_ref, b_ref, c_ref)[slot // SLOTS][slot % SLOTS] = part[:C] + part[C:]


def push_far(far_refs, back, tiles):
    return pl.pallas_call(
        push_far_kernel,
        out_shape=[jax.ShapeDtypeStruct((SLOTS, C, W), f32)] * 3,
        in_specs=[SMEM, VMEM, VMEM],
        out_specs=[VMEM] * 3,
        compiler_params=SMALL,
        cost_estimate=pl.CostEstimate(flops=2 * 12 * W * W * 2 * C, bytes_accessed=4 << 20, transcendentals=0),
    )(far_refs, back, tiles)


def push_kernel(place_ref, back_ref, tiles_ref, diag_ref, *refs):
    outs, held, tiles, out_sems, tile_sems = refs[:10], *refs[10:]
    tile_copies = [pltpu.make_async_copy(tiles_ref.at[i], tiles.at[i], tile_sems.at[i]) for i in range(BLK)]
    for copy in tile_copies:
        copy.start()
    held[...] = jnp.zeros_like(held)
    for i in range(BLK):
        block = jnp.concatenate([back_ref[2 * i, :C], back_ref[2 * i + 1, :C]], axis=1)
        both = jnp.concatenate(split(block), axis=0)
        tile_copies[i].wait()
        for k in range(FAN):
            part = jnp.dot(both, tiles[i, k], preferred_element_type=f32)
            value = part[:C] + part[C:]
            if k == 0:
                diag_ref[i] = value
            else:
                held[place_ref[i * (FAN - 1) + k - 1]] += value
    copies = [pltpu.make_async_copy(held.at[rows], ref, out_sems.at[n]) for n, (rows, ref) in enumerate(places(outs))]
    for copy in copies:
        copy.start()
    for copy in copies:
        copy.wait()


def push(place, back, tiles):
    sizes = (4, 4, 8, 8, 4, 4, 4, 8, 8, 8)
    return pl.pallas_call(
        push_kernel,
        in_specs=[SMEM, VMEM, ANY],
        out_specs=[VMEM] + [ANY] * len(sizes),
        out_shape=[jax.ShapeDtypeStruct((n, C, W), f32) for n in (BLK,) + sizes],
        scratch_shapes=[
            pltpu.VMEM((HELD, C, W), f32),
            pltpu.VMEM((BLK, FAN, W, W), bf16),
            pltpu.SemaphoreType.DMA((len(sizes),)),
            pltpu.SemaphoreType.DMA((BLK,)),
        ],
        compiler_params=PARAMS,
        cost_estimate=pl.CostEstimate(flops=2 * 64 * W * W * 2 * C, bytes_accessed=13 << 20, transcendentals=0),
    )(place, back, tiles)


def add_slots(index_ref, got, group, out_ref):
    per = got[0].shape[0]
    for s in range(3):
        for t in range(SLOTS):
            slot = group * SLOTS + t
            index = index_ref[s * per + slot]
            out_ref[jnp.maximum(index - 1, 0)] += jnp.where(index > 0, got[s][slot], 0.0)


def far_kernel(index_ref, a_ref, b_ref, c_ref, lo_ref, hi_ref, out_lo, out_hi, total):
    total[: BLK // 2] = lo_ref[...]
    total[BLK // 2 :] = hi_ref[...]
    add_slots(index_ref, (a_ref, b_ref, c_ref), 0, total)
    out_lo[...] = total[: BLK // 2]
    out_hi[...] = total[BLK // 2 :]


def mid_kernel(index_ref, a_ref, b_ref, c_ref, up_ref, down_ref, below_ref, above_ref, out_up, out_down):
    half = BLK // 2
    out_up[:half] = up_ref[:half] + below_ref[...]
    out_up[half:] = up_ref[half:]
    out_down[:half] = down_ref[:half]
    out_down[half:] = down_ref[half:] + above_ref[...]
    add_slots(index_ref, (a_ref, b_ref, c_ref), 0, out_up)
    add_slots(index_ref, (a_ref, b_ref, c_ref), 1, out_down)


def near_kernel(index_ref, a_ref, b_ref, c_ref, diag_ref, out):
    out[...] = diag_ref[...]
    add_slots(index_ref, (a_ref, b_ref, c_ref), 0, out)


def gather_sum(kernel, shapes, scratch, index, *args):
    return pl.pallas_call(
        kernel,
        out_shape=[jax.ShapeDtypeStruct((n, C, W), f32) for n in shapes],
        in_specs=[SMEM] + [VMEM] * len(args),
        out_specs=[VMEM] * len(shapes),
        scratch_shapes=scratch,
        compiler_params=SMALL,
        cost_estimate=pl.CostEstimate(flops=12 * C * W, bytes_accessed=3 << 20, transcendentals=0),
    )(index, *args)


def shift(value, axis, size, by):
    return lax.ppermute(value, axis, [(i, (i + by) % size) for i in range(size)])


def over_x(pieces, sign):
    return [shift(piece, "x", NX, sign * (s + 1)) for s, piece in enumerate(pieces)]


def over_col(value):
    return lax.all_to_all(value, COL, 0, 0, tiled=True)


def grad_kernel(core_ref, slope_ref, other_ref, mixed_ref, far_ref, out_ref, wide):
    @pl.when(pl.program_id(0) == 0)
    def _():
        for n, ref in enumerate((mixed_ref, far_ref)):
            hi, lo = split(ref[...])
            for m, value in enumerate((hi, lo, hi)):
                start = (2 * m + n) * CHUNK
                wide[:, start : start + CHUNK] = value

    rows = out_ref.shape[0]
    mine, other = split(slope_ref[...].reshape(rows, CHUNK)), split(other_ref[...])
    left = jnp.concatenate([mine[0], other[0], mine[0], other[0], mine[1], other[1]], axis=1)
    out_ref[...] = lax.dot_general(left, wide[...], (((1,), (1,)), ((), ())), preferred_element_type=f32)


def grad_part(core, slope, other, mixed, mixed_other):
    steps = 4
    rows = 8 * C // steps
    whole = pl.BlockSpec((F, CHUNK), lambda i, s: (0, 0))
    return pl.pallas_call(
        grad_kernel,
        grid_spec=pltpu.PrefetchScalarGridSpec(
            num_scalar_prefetch=1,
            grid=(steps,),
            in_specs=[
                pl.BlockSpec((8 // steps, 1, C, CHUNK), lambda i, s: (i, s[0], 0, 0)),
                pl.BlockSpec((rows, CHUNK), lambda i, s: (i, 0)),
                whole,
                whole,
            ],
            out_specs=pl.BlockSpec((rows, F), lambda i, s: (i, 0)),
            scratch_shapes=[pltpu.VMEM((F, 6 * CHUNK), bf16)],
        ),
        out_shape=jax.ShapeDtypeStruct((8 * C, F), f32),
        compiler_params=PARAMS,
        cost_estimate=pl.CostEstimate(flops=6 * F * F * CHUNK, bytes_accessed=4 << 20, transcendentals=0),
    )(core.reshape(1).astype(jnp.int32), slope.reshape(8, 2, C, CHUNK), other, mixed, mixed_other)


def after(values, others):
    flat, tree = jax.tree.flatten((values, others))
    return jax.tree.unflatten(tree, lax.optimization_barrier(flat))


def on_device(features, neighbours, tiles, weight, cotangent):
    near_at, mid_at, far_at, far_refs, place = tables(neighbours)
    own = features.T.reshape(C, BLK, W).transpose(1, 0, 2)
    me_c = lax.axis_index("c")

    up = shift(own, "zh", NZ, -1)
    down = shift(own, "zh", NZ, 1)
    near = over_x(pick(pick_near_kernel, (4,) * 3, [], near_at, own), 1)
    cot = over_col(cotangent.T.reshape(C, 16, CHUNK).transpose(1, 0, 2)).reshape(F, CHUNK)
    some = far_tiles(far_refs, tiles)
    (up, down), (near, cot, weight_t, some) = after((up, down), (near, cot, weight.T, some))
    weight_t = lax.all_gather(weight_t, COL, axis=0, tiled=True)
    lo, hi, *mid = pick(pick_mid_kernel, (4, 4) + (8,) * 3, [], mid_at, up, down)
    lo = shift(lo, "zh", NZ, -1)
    hi = shift(hi, "zh", NZ, 1)
    mid = over_x(mid, 1)
    lo, hi, mid = lax.optimization_barrier((lo, hi, mid))
    far = pick(pick_far_kernel, (4,) * 3, [pltpu.VMEM((BLK, C, W), f32)], far_at, lo, hi)
    far = over_x(far, 1)
    part = mix(place, own, [lo, hi, up, down, *near, *mid], tiles)
    mixed = mix_far(far_refs, part, far, some)

    mixed = over_col(mixed).reshape(F, CHUNK)
    slope, back = dense(weight_t, mixed, cot)
    back = over_col(back)
    hidden = back[:, C:].transpose(1, 0, 2).reshape(C, 16 * CHUNK).T

    other = lax.dynamic_index_in_dim(slope.reshape(8, 2, C, CHUNK), 1 - me_c, 1, keepdims=False)
    other = shift(other.reshape(8 * C, CHUNK), "c", 2, 1)
    grad = grad_part(me_c, slope, other, mixed, shift(mixed, "c", 2, 1))
    back, grad = after(back, grad)

    far = push_far(far_refs, back, some)
    far = over_x(far, -1)
    grad = lax.all_to_all(grad.reshape(8, C, F), ("y", "zl"), 0, 0, tiled=True)
    diag, lo, hi, up, down, *pieces = push(place, back, tiles)
    near, mid = pieces[:3], pieces[3:]
    far, (mid, hidden) = after(far, (mid, hidden))
    mid = over_x(mid, -1)
    lo, hi = gather_sum(far_kernel, (4, 4), [pltpu.VMEM((BLK, C, W), f32)], far_at, *far, lo, hi)
    lo = shift(lo, "zh", NZ, 1)
    hi = shift(hi, "zh", NZ, -1)
    grad = grad.sum(axis=0).reshape(C, NX, W).transpose(1, 0, 2)
    (mid, lo, hi), (near, grad) = after((mid, lo, hi), (near, grad))
    up, down = gather_sum(mid_kernel, (8, 8), [], mid_at, *mid, up, down, lo, hi)
    (up, down), (near, grad) = after((up, down), (near, grad))
    up = shift(up, "zh", NZ, 1)
    down = shift(down, "zh", NZ, -1)
    near = over_x(near, -1)
    grad = lax.all_to_all(grad, "x", 0, 0, tiled=True).sum(axis=0)
    grad = grad.reshape(2, C // 2, NZ, C).transpose(2, 1, 0, 3).reshape(NZ, C // 2, 2 * C)
    grad = lax.all_to_all(grad, "zh", 0, 0, tiled=True).sum(axis=0)
    (near,) = gather_sum(near_kernel, (8,), [], near_at, *near, diag)
    grad_weight = grad.reshape(C // 2, 2, C).transpose(1, 0, 2).reshape(C, C).T
    grad_features = (near + up + down).transpose(1, 0, 2).reshape(C, BLK * W).T
    return hidden, grad_features, grad_weight


def solution(mesh):
    fine = Mesh(mesh.devices.reshape(4, 4, 4, 2, 2), DOM + COL)
    in_specs = (P(DOM, COL), P(), P(DOM, None, None, None), P(None, COL), P(DOM, COL))
    out_specs = (P(DOM, COL), P(DOM, COL), P(DOM, COL))
    return jax.shard_map(on_device, mesh=fine, in_specs=in_specs, out_specs=out_specs, check_vma=False)
```

```python
import functools

import jax
import jax.numpy as jnp
from jax import lax
from jax.experimental import pallas as pl
from jax.experimental.pallas import tpu as pltpu
from jax.sharding import Mesh
from jax.sharding import PartitionSpec as P

DOM = ("x", "zh")
COL = ("y", "zl", "c")
NX, NZ, NY = 4, 4, 4
BLK, FAN, W, C = 8, 8, 256, 64
HALF = BLK // 2
REFS = BLK * (FAN - 1)
SLOTS = 4
FAR = 60
HELD = FAR + 1
DISTANCES = (2, 1, 3)
F = 1024
CHUNK = 128
f32, bf16 = jnp.float32, jnp.bfloat16
VMEM = pl.BlockSpec(memory_space=pltpu.VMEM)
SMEM = pl.BlockSpec(memory_space=pltpu.SMEM)
ANY = pl.BlockSpec(memory_space=pl.ANY)
PARAMS = pltpu.CompilerParams(vmem_limit_bytes=58 * 2**20)
SMALL = pltpu.CompilerParams(vmem_limit_bytes=10 * 2**20)


def split(value):
    hi = value.astype(bf16)
    lo = (value - hi.astype(f32)).astype(bf16)
    return hi, lo


def tables(neighbours):
    me_x, me_z = lax.axis_index("x"), lax.axis_index("zh")
    rows = neighbours.reshape(NX, NZ, REFS)
    rows = lax.dynamic_index_in_dim(rows, me_z, 1, keepdims=False)
    rows = lax.dynamic_slice_in_dim(jnp.concatenate([rows, rows], axis=0), me_x, NX, 0)
    rows = jnp.stack([rows[s] for s in (0,) + DISTANCES])
    owner, block = rows >> 3, rows & 7
    ref = jnp.arange(REFS)
    same = (owner[:, :, None] == owner[:, None, :]) & (ref[None, :, None] > ref[None, None, :])
    rank = jnp.sum(same.astype(jnp.int32), axis=2)
    wanted = me_x * NZ + ((me_z + jnp.arange(NZ)) & (NZ - 1))
    match = (owner[None, 1:, None, :] == wanted[:, None, None, None]) & (
        rank[None, 1:, None, :] == jnp.arange(SLOTS)[None, None, :, None]
    )
    table = jnp.sum(jnp.where(match, block[None, 1:, None, :] + 1, 0), axis=3)
    e, s = ((owner[0] & 3) - me_z) & 3, (me_x - (owner[0] >> 2)) & 3
    local = jnp.where(e == 2, 0, jnp.where(e == 1, 8, 16)) + block[0]
    start = jnp.where(e == 0, 24, jnp.where(e == 2, 60, 36 + (e >> 1) * 4))
    stride = jnp.where((e & 1) == 1, 8, 4)
    turn = jnp.where(s == 3, 2, jnp.where(s == 1, 1, 0))
    place = jnp.where(s == 0, local, start + turn * stride + rank[0])
    near = table[0].reshape(12)
    mid = jnp.stack([table[1], table[3]], axis=1).reshape(24)
    far = table[2].reshape(12)
    source = ((me_x - jnp.array(DISTANCES)) & 3) * NZ + ((me_z + 2) & 3)
    match = (owner[0][None, None, :] == source[:, None, None]) & (
        rank[0][None, None, :] == jnp.arange(SLOTS)[None, :, None]
    )
    far_refs = jnp.sum(jnp.where(match, ref[None, None, :] + 1, 0), axis=2).reshape(12)
    return near, mid, far, far_refs, jnp.clip(place, 0, FAR)


def pick_slots(index_ref, sources, outs):
    per = outs[0].shape[0]
    for s in range(3):
        for slot in range(per):
            index = jnp.maximum(index_ref[s * per + slot] - 1, 0)
            outs[s][slot] = sources[slot // SLOTS][:, pl.ds(pl.multiple_of(index * W, W), W)]


def pick_near_kernel(index_ref, own_ref, *outs):
    pick_slots(index_ref, (own_ref,), outs)


def pick_mid_kernel(index_ref, up_ref, down_ref, lo_ref, hi_ref, *outs):
    lo_ref[...] = up_ref[:, : HALF * W]
    hi_ref[...] = down_ref[:, HALF * W :]
    pick_slots(index_ref, (up_ref, down_ref), outs)


def pick_far_kernel(index_ref, lo_ref, hi_ref, *refs):
    outs, held = refs[:3], refs[3]
    held[:, : HALF * W] = lo_ref[...]
    held[:, HALF * W :] = hi_ref[...]
    pick_slots(index_ref, (held,), outs)


def pick(kernel, shapes, scratch, index, *sources):
    return pl.pallas_call(
        kernel,
        out_shape=[jax.ShapeDtypeStruct(shape, f32) for shape in shapes],
        in_specs=[SMEM] + [VMEM] * len(sources),
        out_specs=[VMEM] * len(shapes),
        scratch_shapes=scratch,
        compiler_params=SMALL,
        cost_estimate=pl.CostEstimate(flops=0, bytes_accessed=2 << 20, transcendentals=0),
    )(index, *sources)


def places(refs):
    start, pairs = 0, []
    for ref in refs:
        pairs.append((pl.ds(start, ref.shape[0]), ref))
        start += ref.shape[0]
    return pairs


def mixed_kernel(place_ref, own_ref, *refs):
    sources, tiles_ref, out_ref, held, sems = refs[:10], *refs[10:]
    i = pl.program_id(0)

    @pl.when(i == 0)
    def _():
        copies, block = [], 0
        for ref in sources:
            if len(ref.shape) == 3:
                copies.append(pltpu.make_async_copy(ref, held.at[pl.ds(block, ref.shape[0])], sems.at[len(copies)]))
                block += ref.shape[0]
                continue
            for start in range(0, ref.shape[1], W):
                copies.append(pltpu.make_async_copy(ref.at[:, pl.ds(start, W)], held.at[block], sems.at[len(copies)]))
                block += 1
        for copy in copies:
            copy.start()
        held[FAR] = jnp.zeros((C, W), f32)
        for copy in copies:
            copy.wait()

    for j in range(2):
        acc = None
        for k in range(FAN):
            block = own_ref[:, j * W : (j + 1) * W] if k == 0 else held[place_ref[(2 * i + j) * (FAN - 1) + k - 1]]
            part = lax.dot_general(
                jnp.concatenate(split(block), axis=0),
                tiles_ref[j, k],
                (((1,), (1,)), ((), ())),
                preferred_element_type=f32,
            )
            acc = part if acc is None else acc + part
        out_ref[j] = acc[:C] + acc[C:]


def mix(place, own, sources, tiles):
    return pl.pallas_call(
        mixed_kernel,
        grid_spec=pltpu.PrefetchScalarGridSpec(
            num_scalar_prefetch=1,
            grid=(BLK // 2,),
            in_specs=[pl.BlockSpec((C, 2 * W), lambda i, s: (0, i))]
            + [ANY] * len(sources)
            + [pl.BlockSpec((2, FAN, W, W), lambda i, s: (i, 0, 0, 0))],
            out_specs=pl.BlockSpec((2, C, W), lambda i, s: (i, 0, 0)),
            scratch_shapes=[pltpu.VMEM((HELD, C, W), f32), pltpu.SemaphoreType.DMA((30,))],
        ),
        out_shape=jax.ShapeDtypeStruct((BLK, C, W), f32),
        compiler_params=PARAMS,
        cost_estimate=pl.CostEstimate(flops=2 * 64 * W * W * 2 * C, bytes_accessed=13 << 20, transcendentals=0),
    )(place, own, *sources, tiles)


def far_tiles_kernel(refs_ref, tiles_ref, out_ref, sems):
    copies = []
    for slot in range(12):
        ref = jnp.maximum(refs_ref[slot] - 1, 0)
        i = ref // (FAN - 1)
        copies.append(
            pltpu.make_async_copy(tiles_ref.at[i, ref - i * (FAN - 1) + 1], out_ref.at[slot], sems.at[slot])
        )
    for copy in copies:
        copy.start()
    for copy in copies:
        copy.wait()


def far_tiles(far_refs, tiles):
    return pl.pallas_call(
        far_tiles_kernel,
        out_shape=jax.ShapeDtypeStruct((12, W, W), bf16),
        in_specs=[SMEM, ANY],
        out_specs=VMEM,
        scratch_shapes=[pltpu.SemaphoreType.DMA((12,))],
        compiler_params=PARAMS,
        cost_estimate=pl.CostEstimate(flops=0, bytes_accessed=3 << 20, transcendentals=0),
    )(far_refs, tiles)


def mix_far_kernel(refs_ref, part_ref, a_ref, b_ref, c_ref, tiles_ref, out_ref, total):
    total[...] = part_ref[...]
    for slot in range(12):
        both = jnp.concatenate(split((a_ref, b_ref, c_ref)[slot // SLOTS][slot % SLOTS]), axis=0)
        part = lax.dot_general(both, tiles_ref[slot], (((1,), (1,)), ((), ())), preferred_element_type=f32)
        ref = refs_ref[slot]
        total[jnp.maximum(ref - 1, 0) // (FAN - 1)] += jnp.where(ref > 0, part[:C] + part[C:], 0.0)
    for i in range(BLK):
        out_ref[2 * i] = total[i, :, :CHUNK]
        out_ref[2 * i + 1] = total[i, :, CHUNK:]


def mix_far(far_refs, part, far, tiles):
    return pl.pallas_call(
        mix_far_kernel,
        out_shape=jax.ShapeDtypeStruct((16, C, CHUNK), f32),
        in_specs=[SMEM] + [VMEM] * 5,
        out_specs=VMEM,
        scratch_shapes=[pltpu.VMEM((BLK, C, W), f32)],
        compiler_params=SMALL,
        cost_estimate=pl.CostEstimate(flops=2 * 12 * W * W * 2 * C, bytes_accessed=4 << 20, transcendentals=0),
    )(far_refs, part, *far, tiles)


def dense_kernel(weight_ref, mixed_ref, cot_ref, rows_ref, back_ref, held, sems):
    step = F // 2
    copies = []
    for j in range(F // step):
        rows = pl.ds(j * step, step)
        copies.append(pltpu.make_async_copy(weight_ref.at[rows], held.at[rows], sems.at[j]))
    for copy in copies:
        copy.start()
    mhi, mlo = split(mixed_ref[...])
    parts = jnp.concatenate([mhi, mlo], axis=1)
    back = None
    for j, copy in enumerate(copies):
        rows = pl.ds(j * step, step)
        copy.wait()
        whi, wlo = split(held[rows])
        both = jnp.dot(whi, parts, preferred_element_type=f32)
        low = jnp.dot(wlo, mhi, preferred_element_type=f32)
        pre = both[:, :CHUNK] + (both[:, CHUNK:] + low)
        sig = jax.nn.sigmoid(pre)
        rows_ref[rows, CHUNK:] = pre * sig
        slope = cot_ref[rows] * sig * (1.0 + pre * (1.0 - sig))
        rows_ref[rows, :CHUNK] = slope
        shi, slo = split(slope.T)
        both = jnp.dot(jnp.concatenate([shi, slo], axis=0), whi, preferred_element_type=f32)
        low = jnp.dot(shi, wlo, preferred_element_type=f32)
        part = both[:CHUNK] + (both[CHUNK:] + low)
        back = part if back is None else back + part
    back_ref[...] = back.T.reshape(16, C, CHUNK)


def dense(weight_t, mixed, cot):
    return pl.pallas_call(
        dense_kernel,
        in_specs=[ANY, VMEM, VMEM],
        out_specs=[VMEM, VMEM],
        out_shape=[jax.ShapeDtypeStruct((F, 2 * CHUNK), f32), jax.ShapeDtypeStruct((16, C, CHUNK), f32)],
        scratch_shapes=[pltpu.VMEM((F, F), f32), pltpu.SemaphoreType.DMA((2,))],
        compiler_params=PARAMS,
        cost_estimate=pl.CostEstimate(flops=12 * F * F * CHUNK, bytes_accessed=8 << 20, transcendentals=F * CHUNK),
    )(weight_t, mixed, cot)


def push_far_kernel(refs_ref, back_ref, tiles_ref, a_ref, b_ref, c_ref):
    for slot in range(12):
        i = jnp.maximum(refs_ref[slot] - 1, 0) // (FAN - 1)
        block = jnp.concatenate([back_ref[2 * i], back_ref[2 * i + 1]], axis=1)
        both = jnp.concatenate(split(block), axis=0)
        part = jnp.dot(both, tiles_ref[slot], preferred_element_type=f32)
        (a_ref, b_ref, c_ref)[slot // SLOTS][slot % SLOTS] = part[:C] + part[C:]


def push_far(far_refs, back, tiles):
    return pl.pallas_call(
        push_far_kernel,
        out_shape=[jax.ShapeDtypeStruct((SLOTS, C, W), f32)] * 3,
        in_specs=[SMEM, VMEM, VMEM],
        out_specs=[VMEM] * 3,
        compiler_params=SMALL,
        cost_estimate=pl.CostEstimate(flops=2 * 12 * W * W * 2 * C, bytes_accessed=4 << 20, transcendentals=0),
    )(far_refs, back, tiles)


def push_kernel(place_ref, back_ref, tiles_ref, diag_ref, *refs):
    outs, held, tiles, out_sems, tile_sems = refs[:10], *refs[10:]
    tile_copies = [pltpu.make_async_copy(tiles_ref.at[i], tiles.at[i], tile_sems.at[i]) for i in range(BLK)]
    for copy in tile_copies:
        copy.start()
    held[...] = jnp.zeros_like(held)
    for i in range(BLK):
        block = jnp.concatenate([back_ref[2 * i], back_ref[2 * i + 1]], axis=1)
        both = jnp.concatenate(split(block), axis=0)
        tile_copies[i].wait()
        for k in range(FAN):
            part = jnp.dot(both, tiles[i, k], preferred_element_type=f32)
            value = part[:C] + part[C:]
            if k == 0:
                diag_ref[i] = value
            else:
                held[place_ref[i * (FAN - 1) + k - 1]] += value
    copies = [pltpu.make_async_copy(held.at[rows], ref, out_sems.at[n]) for n, (rows, ref) in enumerate(places(outs))]
    for copy in copies:
        copy.start()
    for copy in copies:
        copy.wait()


def push(place, back, tiles):
    sizes = (4, 4, 8, 8, 4, 4, 4, 8, 8, 8)
    return pl.pallas_call(
        push_kernel,
        in_specs=[SMEM, VMEM, ANY],
        out_specs=[VMEM] + [ANY] * len(sizes),
        out_shape=[jax.ShapeDtypeStruct((n, C, W), f32) for n in (BLK,) + sizes],
        scratch_shapes=[
            pltpu.VMEM((HELD, C, W), f32),
            pltpu.VMEM((BLK, FAN, W, W), bf16),
            pltpu.SemaphoreType.DMA((len(sizes),)),
            pltpu.SemaphoreType.DMA((BLK,)),
        ],
        compiler_params=PARAMS,
        cost_estimate=pl.CostEstimate(flops=2 * 64 * W * W * 2 * C, bytes_accessed=13 << 20, transcendentals=0),
    )(place, back, tiles)


def add_slots(index_ref, got, group, out_ref):
    per = got[0].shape[0]
    for s in range(3):
        for t in range(SLOTS):
            slot = group * SLOTS + t
            index = index_ref[s * per + slot]
            out_ref[jnp.maximum(index - 1, 0)] += jnp.where(index > 0, got[s][slot], 0.0)


def far_kernel(index_ref, a_ref, b_ref, c_ref, lo_ref, hi_ref, out_lo, out_hi, total):
    total[: BLK // 2] = lo_ref[...]
    total[BLK // 2 :] = hi_ref[...]
    add_slots(index_ref, (a_ref, b_ref, c_ref), 0, total)
    out_lo[...] = total[: BLK // 2]
    out_hi[...] = total[BLK // 2 :]


def mid_kernel(index_ref, a_ref, b_ref, c_ref, up_ref, down_ref, below_ref, above_ref, out_up, out_down):
    half = BLK // 2
    out_up[:half] = up_ref[:half] + below_ref[...]
    out_up[half:] = up_ref[half:]
    out_down[:half] = down_ref[:half]
    out_down[half:] = down_ref[half:] + above_ref[...]
    add_slots(index_ref, (a_ref, b_ref, c_ref), 0, out_up)
    add_slots(index_ref, (a_ref, b_ref, c_ref), 1, out_down)


def near_kernel(index_ref, a_ref, b_ref, c_ref, diag_ref, out):
    out[...] = diag_ref[...]
    add_slots(index_ref, (a_ref, b_ref, c_ref), 0, out)


def gather_sum(kernel, shapes, scratch, index, *args):
    return pl.pallas_call(
        kernel,
        out_shape=[jax.ShapeDtypeStruct((n, C, W), f32) for n in shapes],
        in_specs=[SMEM] + [VMEM] * len(args),
        out_specs=[VMEM] * len(shapes),
        scratch_shapes=scratch,
        compiler_params=SMALL,
        cost_estimate=pl.CostEstimate(flops=12 * C * W, bytes_accessed=3 << 20, transcendentals=0),
    )(index, *args)


def shift(value, axis, size, by):
    return lax.ppermute(value, axis, [(i, (i + by) % size) for i in range(size)])


def over_x(pieces, sign):
    return [shift(piece, "x", NX, sign * s) for s, piece in zip(DISTANCES, pieces)]


def over_col(value):
    return lax.all_to_all(value, COL, 0, 0, tiled=True)


def grad_kernel(core_ref, mine_ref, other_ref, mixed_ref, far_ref, out_ref, wide):
    @pl.when(pl.program_id(0) == 0)
    def _():
        for n, ref in enumerate((mixed_ref, far_ref)):
            hi, lo = split(ref[...])
            for m, value in enumerate((hi, lo, hi)):
                start = (2 * m + n) * CHUNK
                wide[:, start : start + CHUNK] = value

    parts = out_ref.shape[0]
    mine = mine_ref[...].reshape(parts * C, 2 * CHUNK)
    other = other_ref[...]
    (ahi, alo), (bhi, blo) = split(mine[:, :CHUNK]), split(other[:, :CHUNK])
    left = jnp.concatenate([ahi, bhi, ahi, bhi, alo, blo], axis=1)
    value = lax.dot_general(left, wide[...], (((1,), (1,)), ((), ())), preferred_element_type=f32)
    out_ref[:, :, :F] = value.reshape(parts, C, F)
    low = core_ref[0] == 0
    mine, other = mine[:, CHUNK:], other[:, CHUNK:]
    out_ref[:, :, F : F + CHUNK] = jnp.where(low, mine, other).reshape(parts, C, CHUNK)
    out_ref[:, :, F + CHUNK :] = jnp.where(low, other, mine).reshape(parts, C, CHUNK)


def grad_part(core, mine, other, mixed, mixed_other):
    steps = 4
    whole = pl.BlockSpec((F, CHUNK), lambda i, s: (0, 0))
    return pl.pallas_call(
        grad_kernel,
        grid_spec=pltpu.PrefetchScalarGridSpec(
            num_scalar_prefetch=1,
            grid=(steps,),
            in_specs=[
                pl.BlockSpec((8 // steps, 1, C, 2 * CHUNK), lambda i, s: (i, s[0], 0, 0)),
                pl.BlockSpec((8 * C // steps, 2 * CHUNK), lambda i, s: (i, 0)),
                whole,
                whole,
            ],
            out_specs=pl.BlockSpec((8 // steps, C, F + 2 * CHUNK), lambda i, s: (i, 0, 0)),
            scratch_shapes=[pltpu.VMEM((F, 6 * CHUNK), bf16)],
        ),
        out_shape=jax.ShapeDtypeStruct((8, C, F + 2 * CHUNK), f32),
        compiler_params=PARAMS,
        cost_estimate=pl.CostEstimate(flops=6 * F * F * CHUNK, bytes_accessed=4 << 20, transcendentals=0),
    )(core.reshape(1).astype(jnp.int32), mine, other, mixed, mixed_other)


def after(values, others):
    flat, tree = jax.tree.flatten((values, others))
    return jax.tree.unflatten(tree, lax.optimization_barrier(flat))


def on_device(features, neighbours, tiles, weight, cotangent):
    near_at, mid_at, far_at, far_refs, place = tables(neighbours)
    own = features.T
    me_c = lax.axis_index("c")

    up = shift(own, "zh", NZ, -1)
    down = shift(own, "zh", NZ, 1)
    near = over_x(pick(pick_near_kernel, ((4, C, W),) * 3, [], near_at, own), 1)
    cot = over_col(cotangent.T.reshape(C, 16, CHUNK).transpose(1, 0, 2)).reshape(F, CHUNK)
    some = far_tiles(far_refs, tiles)
    (up, down), (near, cot, weight_t, some) = after((up, down), (near, cot, weight.T, some))
    weight_t = lax.all_gather(weight_t, COL, axis=0, tiled=True)
    lo, hi, *mid = pick(pick_mid_kernel, ((C, HALF * W),) * 2 + ((8, C, W),) * 3, [], mid_at, up, down)
    lo = shift(lo, "zh", NZ, -1)
    hi = shift(hi, "zh", NZ, 1)
    mid = over_x(mid, 1)
    lo, hi, mid = lax.optimization_barrier((lo, hi, mid))
    far = pick(pick_far_kernel, ((4, C, W),) * 3, [pltpu.VMEM((C, BLK * W), f32)], far_at, lo, hi)
    far = over_x(far, 1)
    part = mix(place, own, [lo, hi, up, down, *near, *mid], tiles)
    mixed = mix_far(far_refs, part, far, some)

    mixed = over_col(mixed).reshape(F, CHUNK)
    rows, back = dense(weight_t, mixed, cot)
    back = over_col(back)

    rows = rows.reshape(8, 2, C, 2 * CHUNK)
    other = lax.dynamic_index_in_dim(rows, 1 - me_c, 1, keepdims=False)
    other = shift(other.reshape(8 * C, 2 * CHUNK), "c", 2, 1)
    grad = grad_part(me_c, rows, other, mixed, shift(mixed, "c", 2, 1))
    back, grad = after(back, grad)

    far = push_far(far_refs, back, some)
    far = over_x(far, -1)
    grad = lax.all_to_all(grad, ("y", "zl"), 0, 0, tiled=True)
    diag, lo, hi, up, down, *pieces = push(place, back, tiles)
    near, mid = pieces[:3], pieces[3:]
    far, mid = after(far, mid)
    mid = over_x(mid, -1)
    lo, hi = gather_sum(far_kernel, (4, 4), [pltpu.VMEM((BLK, C, W), f32)], far_at, *far, lo, hi)
    lo = shift(lo, "zh", NZ, 1)
    hi = shift(hi, "zh", NZ, -1)
    hidden = grad[:, :, F:].transpose(1, 0, 2).reshape(C, 16 * CHUNK).T
    grad = grad[:, :, :F].sum(axis=0).reshape(C, NX, W).transpose(1, 0, 2)
    (mid, lo, hi), (near, grad) = after((mid, lo, hi), (near, grad))
    up, down = gather_sum(mid_kernel, (8, 8), [], mid_at, *mid, up, down, lo, hi)
    (up, down), (near, grad) = after((up, down), (near, grad))
    up = shift(up, "zh", NZ, 1)
    down = shift(down, "zh", NZ, -1)
    near = over_x(near, -1)
    grad = lax.all_to_all(grad, "x", 0, 0, tiled=True).sum(axis=0)
    grad = grad.reshape(2, C // 2, NZ, C).transpose(2, 1, 0, 3).reshape(NZ, C // 2, 2 * C)
    grad = lax.all_to_all(grad, "zh", 0, 0, tiled=True).sum(axis=0)
    (near,) = gather_sum(near_kernel, (8,), [], near_at, *near, diag)
    grad_weight = grad.reshape(C // 2, 2, C).transpose(1, 0, 2).reshape(C, C).T
    grad_features = (near + up + down).transpose(1, 0, 2).reshape(C, BLK * W).T
    return hidden, grad_features, grad_weight


def solution(mesh):
    fine = Mesh(mesh.devices.reshape(4, 4, 4, 2, 2), DOM + COL)
    in_specs = (P(DOM, COL), P(), P(DOM, None, None, None), P(None, COL), P(DOM, COL))
    out_specs = (P(DOM, COL), P(DOM, COL), P(DOM, COL))
    return jax.shard_map(on_device, mesh=fine, in_specs=in_specs, out_specs=out_specs, check_vma=False)
```

```python
import functools

import jax
import jax.numpy as jnp
from jax import lax
from jax.experimental import pallas as pl
from jax.experimental.pallas import tpu as pltpu
from jax.sharding import Mesh
from jax.sharding import PartitionSpec as P

DOM = ("x", "zh")
COL = ("y", "zl", "c")
NX, NZ, NY = 4, 4, 4
BLK, FAN, W, C = 8, 8, 256, 64
HALF = BLK // 2
REFS = BLK * (FAN - 1)
SLOTS = 4
FAR = 60
HELD = FAR + 1
DISTANCES = (2, 1, 3)
F = 1024
CHUNK = 128
f32, bf16 = jnp.float32, jnp.bfloat16
VMEM = pl.BlockSpec(memory_space=pltpu.VMEM)
SMEM = pl.BlockSpec(memory_space=pltpu.SMEM)
ANY = pl.BlockSpec(memory_space=pl.ANY)
PARAMS = pltpu.CompilerParams(vmem_limit_bytes=58 * 2**20)
SMALL = pltpu.CompilerParams(vmem_limit_bytes=10 * 2**20)


def split(value):
    hi = value.astype(bf16)
    lo = (value - hi.astype(f32)).astype(bf16)
    return hi, lo


def tables(neighbours):
    me_x, me_z = lax.axis_index("x"), lax.axis_index("zh")
    rows = neighbours.reshape(NX, NZ, REFS)
    rows = lax.dynamic_index_in_dim(rows, me_z, 1, keepdims=False)
    rows = lax.dynamic_slice_in_dim(jnp.concatenate([rows, rows], axis=0), me_x, NX, 0)
    rows = jnp.stack([rows[s] for s in (0,) + DISTANCES])
    owner, block = rows >> 3, rows & 7
    ref = jnp.arange(REFS)
    same = (owner[:, :, None] == owner[:, None, :]) & (ref[None, :, None] > ref[None, None, :])
    rank = jnp.sum(same.astype(jnp.int32), axis=2)
    wanted = me_x * NZ + ((me_z + jnp.arange(NZ)) & (NZ - 1))
    match = (owner[None, 1:, None, :] == wanted[:, None, None, None]) & (
        rank[None, 1:, None, :] == jnp.arange(SLOTS)[None, None, :, None]
    )
    table = jnp.sum(jnp.where(match, block[None, 1:, None, :] + 1, 0), axis=3)
    e, s = ((owner[0] & 3) - me_z) & 3, (me_x - (owner[0] >> 2)) & 3
    local = jnp.where(e == 2, 0, jnp.where(e == 1, 8, 16)) + block[0]
    start = jnp.where(e == 0, 24, jnp.where(e == 2, 60, 36 + (e >> 1) * 4))
    stride = jnp.where((e & 1) == 1, 8, 4)
    turn = jnp.where(s == 3, 2, jnp.where(s == 1, 1, 0))
    place = jnp.where(s == 0, local, start + turn * stride + rank[0])
    near = table[0].reshape(12)
    mid = jnp.stack([table[1], table[3]], axis=1).reshape(24)
    far = table[2].reshape(12)
    source = ((me_x - jnp.array(DISTANCES)) & 3) * NZ + ((me_z + 2) & 3)
    match = (owner[0][None, None, :] == source[:, None, None]) & (
        rank[0][None, None, :] == jnp.arange(SLOTS)[None, :, None]
    )
    far_refs = jnp.sum(jnp.where(match, ref[None, None, :] + 1, 0), axis=2).reshape(12)
    return near, mid, far, far_refs, jnp.clip(place, 0, FAR)


def pick_slots(index_ref, sources, outs):
    per = outs[0].shape[0]
    for s in range(3):
        for slot in range(per):
            index = jnp.maximum(index_ref[s * per + slot] - 1, 0)
            outs[s][slot] = sources[slot // SLOTS][:, pl.ds(pl.multiple_of(index * W, W), W)]


def pick_near_kernel(index_ref, own_ref, *outs):
    pick_slots(index_ref, (own_ref,), outs)


def pick_mid_kernel(index_ref, up_ref, down_ref, lo_ref, hi_ref, *outs):
    lo_ref[...] = up_ref[:, : HALF * W]
    hi_ref[...] = down_ref[:, HALF * W :]
    pick_slots(index_ref, (up_ref, down_ref), outs)


def pick_far_kernel(index_ref, lo_ref, hi_ref, *refs):
    outs, held = refs[:3], refs[3]
    held[:, : HALF * W] = lo_ref[...]
    held[:, HALF * W :] = hi_ref[...]
    pick_slots(index_ref, (held,), outs)


def pick(kernel, shapes, scratch, index, *sources):
    return pl.pallas_call(
        kernel,
        out_shape=[jax.ShapeDtypeStruct(shape, f32) for shape in shapes],
        in_specs=[SMEM] + [VMEM] * len(sources),
        out_specs=[VMEM] * len(shapes),
        scratch_shapes=scratch,
        compiler_params=SMALL,
        cost_estimate=pl.CostEstimate(flops=0, bytes_accessed=2 << 20, transcendentals=0),
    )(index, *sources)


def places(refs):
    start, pairs = 0, []
    for ref in refs:
        pairs.append((pl.ds(start, ref.shape[0]), ref))
        start += ref.shape[0]
    return pairs


def mixed_kernel(place_ref, own_ref, *refs):
    sources, tiles_ref, out_ref, held, sems = refs[:10], *refs[10:]
    i = pl.program_id(0)

    @pl.when(i == 0)
    def _():
        copies, block = [], 0
        for ref in sources:
            if len(ref.shape) == 3:
                copies.append(pltpu.make_async_copy(ref, held.at[pl.ds(block, ref.shape[0])], sems.at[len(copies)]))
                block += ref.shape[0]
                continue
            for start in range(0, ref.shape[1], W):
                copies.append(pltpu.make_async_copy(ref.at[:, pl.ds(start, W)], held.at[block], sems.at[len(copies)]))
                block += 1
        for copy in copies:
            copy.start()
        held[FAR] = jnp.zeros((C, W), f32)
        for copy in copies:
            copy.wait()

    for j in range(2):
        acc = None
        for k in range(FAN):
            block = own_ref[:, j * W : (j + 1) * W] if k == 0 else held[place_ref[(2 * i + j) * (FAN - 1) + k - 1]]
            part = lax.dot_general(
                jnp.concatenate(split(block), axis=0),
                tiles_ref[j, k],
                (((1,), (1,)), ((), ())),
                preferred_element_type=f32,
            )
            acc = part if acc is None else acc + part
        out_ref[j] = acc[:C] + acc[C:]


def mix(place, own, sources, tiles):
    return pl.pallas_call(
        mixed_kernel,
        grid_spec=pltpu.PrefetchScalarGridSpec(
            num_scalar_prefetch=1,
            grid=(BLK // 2,),
            in_specs=[pl.BlockSpec((C, 2 * W), lambda i, s: (0, i))]
            + [ANY] * len(sources)
            + [pl.BlockSpec((2, FAN, W, W), lambda i, s: (i, 0, 0, 0))],
            out_specs=pl.BlockSpec((2, C, W), lambda i, s: (i, 0, 0)),
            scratch_shapes=[pltpu.VMEM((HELD, C, W), f32), pltpu.SemaphoreType.DMA((30,))],
        ),
        out_shape=jax.ShapeDtypeStruct((BLK, C, W), f32),
        compiler_params=PARAMS,
        cost_estimate=pl.CostEstimate(flops=2 * 64 * W * W * 2 * C, bytes_accessed=13 << 20, transcendentals=0),
    )(place, own, *sources, tiles)


def far_tiles_kernel(refs_ref, tiles_ref, out_ref, sems):
    copies = []
    for slot in range(12):
        ref = jnp.maximum(refs_ref[slot] - 1, 0)
        i = ref // (FAN - 1)
        copies.append(
            pltpu.make_async_copy(tiles_ref.at[i, ref - i * (FAN - 1) + 1], out_ref.at[slot], sems.at[slot])
        )
    for copy in copies:
        copy.start()
    for copy in copies:
        copy.wait()


def far_tiles(far_refs, tiles):
    return pl.pallas_call(
        far_tiles_kernel,
        out_shape=jax.ShapeDtypeStruct((12, W, W), bf16),
        in_specs=[SMEM, ANY],
        out_specs=VMEM,
        scratch_shapes=[pltpu.SemaphoreType.DMA((12,))],
        compiler_params=PARAMS,
        cost_estimate=pl.CostEstimate(flops=0, bytes_accessed=3 << 20, transcendentals=0),
    )(far_refs, tiles)


def mix_far_kernel(refs_ref, part_ref, a_ref, b_ref, c_ref, tiles_ref, out_ref, total):
    total[...] = part_ref[...]
    for slot in range(12):
        both = jnp.concatenate(split((a_ref, b_ref, c_ref)[slot // SLOTS][slot % SLOTS]), axis=0)
        part = lax.dot_general(both, tiles_ref[slot], (((1,), (1,)), ((), ())), preferred_element_type=f32)
        ref = refs_ref[slot]
        total[jnp.maximum(ref - 1, 0) // (FAN - 1)] += jnp.where(ref > 0, part[:C] + part[C:], 0.0)
    for i in range(BLK):
        out_ref[2 * i] = total[i, :, :CHUNK]
        out_ref[2 * i + 1] = total[i, :, CHUNK:]


def mix_far(far_refs, part, far, tiles):
    return pl.pallas_call(
        mix_far_kernel,
        out_shape=jax.ShapeDtypeStruct((16, C, CHUNK), f32),
        in_specs=[SMEM] + [VMEM] * 5,
        out_specs=VMEM,
        scratch_shapes=[pltpu.VMEM((BLK, C, W), f32)],
        compiler_params=SMALL,
        cost_estimate=pl.CostEstimate(flops=2 * 12 * W * W * 2 * C, bytes_accessed=4 << 20, transcendentals=0),
    )(far_refs, part, *far, tiles)


def dense_kernel(weight_ref, mixed_ref, zl_ref, mine_ref, other_ref, rows_ref, back_ref, held, sems):
    step = F // 2
    copies = []
    for j in range(F // step):
        rows = pl.ds(j * step, step)
        copies.append(pltpu.make_async_copy(weight_ref.at[rows], held.at[rows], sems.at[j]))
    for copy in copies:
        copy.start()
    mhi, mlo = split(mixed_ref[...])
    parts = jnp.concatenate([mhi, mlo], axis=1)
    back = None
    for j, copy in enumerate(copies):
        rows = pl.ds(j * step, step)
        copy.wait()
        whi, wlo = split(held[rows])
        both = jnp.dot(whi, parts, preferred_element_type=f32)
        low = jnp.dot(wlo, mhi, preferred_element_type=f32)
        pre = both[:, :CHUNK] + (both[:, CHUNK:] + low)
        sig = jax.nn.sigmoid(pre)
        rows_ref[rows, CHUNK:] = pre * sig
        pairs = []
        for part in range(j * step // (2 * C), (j + 1) * step // (2 * C)):
            y, zl = part // 2, part % 2
            own = zl_ref[0] == zl
            pairs += [jnp.where(own, mine_ref[2 * y + c], other_ref[2 * y + c]) for c in range(2)]
        slope = jnp.concatenate(pairs, axis=0) * sig * (1.0 + pre * (1.0 - sig))
        rows_ref[rows, :CHUNK] = slope
        shi, slo = split(slope.T)
        both = jnp.dot(jnp.concatenate([shi, slo], axis=0), whi, preferred_element_type=f32)
        low = jnp.dot(shi, wlo, preferred_element_type=f32)
        part = both[:CHUNK] + (both[CHUNK:] + low)
        back = part if back is None else back + part
    back_ref[...] = back.T.reshape(16, C, CHUNK)


def dense(weight_t, mixed, me_l, cot_mine, cot_other):
    return pl.pallas_call(
        dense_kernel,
        in_specs=[ANY, VMEM, SMEM, VMEM, VMEM],
        out_specs=[VMEM, VMEM],
        out_shape=[jax.ShapeDtypeStruct((F, 2 * CHUNK), f32), jax.ShapeDtypeStruct((16, C, CHUNK), f32)],
        scratch_shapes=[pltpu.VMEM((F, F), f32), pltpu.SemaphoreType.DMA((2,))],
        compiler_params=PARAMS,
        cost_estimate=pl.CostEstimate(flops=12 * F * F * CHUNK, bytes_accessed=8 << 20, transcendentals=F * CHUNK),
    )(weight_t, mixed, me_l.reshape(1).astype(jnp.int32), cot_mine, cot_other)


def push_far_kernel(refs_ref, back_ref, tiles_ref, a_ref, b_ref, c_ref):
    for slot in range(12):
        i = jnp.maximum(refs_ref[slot] - 1, 0) // (FAN - 1)
        block = jnp.concatenate([back_ref[2 * i], back_ref[2 * i + 1]], axis=1)
        both = jnp.concatenate(split(block), axis=0)
        part = jnp.dot(both, tiles_ref[slot], preferred_element_type=f32)
        (a_ref, b_ref, c_ref)[slot // SLOTS][slot % SLOTS] = part[:C] + part[C:]


def push_far(far_refs, back, tiles):
    return pl.pallas_call(
        push_far_kernel,
        out_shape=[jax.ShapeDtypeStruct((SLOTS, C, W), f32)] * 3,
        in_specs=[SMEM, VMEM, VMEM],
        out_specs=[VMEM] * 3,
        compiler_params=SMALL,
        cost_estimate=pl.CostEstimate(flops=2 * 12 * W * W * 2 * C, bytes_accessed=4 << 20, transcendentals=0),
    )(far_refs, back, tiles)


def push_kernel(place_ref, back_ref, tiles_ref, diag_ref, *refs):
    outs, held, tiles, out_sems, tile_sems = refs[:10], *refs[10:]
    tile_copies = [pltpu.make_async_copy(tiles_ref.at[i], tiles.at[i], tile_sems.at[i]) for i in range(BLK)]
    for copy in tile_copies:
        copy.start()
    held[...] = jnp.zeros_like(held)
    for i in range(BLK):
        block = jnp.concatenate([back_ref[2 * i], back_ref[2 * i + 1]], axis=1)
        both = jnp.concatenate(split(block), axis=0)
        tile_copies[i].wait()
        for k in range(FAN):
            part = jnp.dot(both, tiles[i, k], preferred_element_type=f32)
            value = part[:C] + part[C:]
            if k == 0:
                diag_ref[i] = value
            else:
                held[place_ref[i * (FAN - 1) + k - 1]] += value
    copies = [pltpu.make_async_copy(held.at[rows], ref, out_sems.at[n]) for n, (rows, ref) in enumerate(places(outs))]
    for copy in copies:
        copy.start()
    for copy in copies:
        copy.wait()


def push(place, back, tiles):
    sizes = (4, 4, 8, 8, 4, 4, 4, 8, 8, 8)
    return pl.pallas_call(
        push_kernel,
        in_specs=[SMEM, VMEM, ANY],
        out_specs=[VMEM] + [ANY] * len(sizes),
        out_shape=[jax.ShapeDtypeStruct((n, C, W), f32) for n in (BLK,) + sizes],
        scratch_shapes=[
            pltpu.VMEM((HELD, C, W), f32),
            pltpu.VMEM((BLK, FAN, W, W), bf16),
            pltpu.SemaphoreType.DMA((len(sizes),)),
            pltpu.SemaphoreType.DMA((BLK,)),
        ],
        compiler_params=PARAMS,
        cost_estimate=pl.CostEstimate(flops=2 * 64 * W * W * 2 * C, bytes_accessed=13 << 20, transcendentals=0),
    )(place, back, tiles)


def add_slots(index_ref, got, group, out_ref):
    per = got[0].shape[0]
    for s in range(3):
        for t in range(SLOTS):
            slot = group * SLOTS + t
            index = index_ref[s * per + slot]
            out_ref[jnp.maximum(index - 1, 0)] += jnp.where(index > 0, got[s][slot], 0.0)


def far_kernel(index_ref, a_ref, b_ref, c_ref, lo_ref, hi_ref, out_lo, out_hi, total):
    total[: BLK // 2] = lo_ref[...]
    total[BLK // 2 :] = hi_ref[...]
    add_slots(index_ref, (a_ref, b_ref, c_ref), 0, total)
    out_lo[...] = total[: BLK // 2]
    out_hi[...] = total[BLK // 2 :]


def mid_kernel(index_ref, a_ref, b_ref, c_ref, up_ref, down_ref, below_ref, above_ref, out_up, out_down):
    half = BLK // 2
    out_up[:half] = up_ref[:half] + below_ref[...]
    out_up[half:] = up_ref[half:]
    out_down[:half] = down_ref[:half]
    out_down[half:] = down_ref[half:] + above_ref[...]
    add_slots(index_ref, (a_ref, b_ref, c_ref), 0, out_up)
    add_slots(index_ref, (a_ref, b_ref, c_ref), 1, out_down)


def near_kernel(index_ref, a_ref, b_ref, c_ref, diag_ref, out):
    out[...] = diag_ref[...]
    add_slots(index_ref, (a_ref, b_ref, c_ref), 0, out)


def gather_sum(kernel, shapes, scratch, index, *args):
    return pl.pallas_call(
        kernel,
        out_shape=[jax.ShapeDtypeStruct((n, C, W), f32) for n in shapes],
        in_specs=[SMEM] + [VMEM] * len(args),
        out_specs=[VMEM] * len(shapes),
        scratch_shapes=scratch,
        compiler_params=SMALL,
        cost_estimate=pl.CostEstimate(flops=12 * C * W, bytes_accessed=3 << 20, transcendentals=0),
    )(index, *args)


def shift(value, axis, size, by):
    return lax.ppermute(value, axis, [(i, (i + by) % size) for i in range(size)])


def over_x(pieces, sign):
    return [shift(piece, "x", NX, sign * s) for s, piece in zip(DISTANCES, pieces)]


def over_col(value):
    return lax.all_to_all(value, COL, 0, 0, tiled=True)


def grad_kernel(core_ref, mine_ref, other_ref, mixed_ref, far_ref, out_ref, wide):
    @pl.when(pl.program_id(0) == 0)
    def _():
        for n, ref in enumerate((mixed_ref, far_ref)):
            hi, lo = split(ref[...])
            for m, value in enumerate((hi, lo, hi)):
                start = (2 * m + n) * CHUNK
                wide[:, start : start + CHUNK] = value

    parts = out_ref.shape[0]
    mine = mine_ref[...].reshape(parts * C, 2 * CHUNK)
    other = other_ref[...]
    (ahi, alo), (bhi, blo) = split(mine[:, :CHUNK]), split(other[:, :CHUNK])
    left = jnp.concatenate([ahi, bhi, ahi, bhi, alo, blo], axis=1)
    value = lax.dot_general(left, wide[...], (((1,), (1,)), ((), ())), preferred_element_type=f32)
    out_ref[:, :, :F] = value.reshape(parts, C, F)
    low = core_ref[0] == 0
    mine, other = mine[:, CHUNK:], other[:, CHUNK:]
    out_ref[:, :, F : F + CHUNK] = jnp.where(low, mine, other).reshape(parts, C, CHUNK)
    out_ref[:, :, F + CHUNK :] = jnp.where(low, other, mine).reshape(parts, C, CHUNK)


def grad_part(core, mine, other, mixed, mixed_other):
    steps = 4
    whole = pl.BlockSpec((F, CHUNK), lambda i, s: (0, 0))
    return pl.pallas_call(
        grad_kernel,
        grid_spec=pltpu.PrefetchScalarGridSpec(
            num_scalar_prefetch=1,
            grid=(steps,),
            in_specs=[
                pl.BlockSpec((8 // steps, 1, C, 2 * CHUNK), lambda i, s: (i, s[0], 0, 0)),
                pl.BlockSpec((8 * C // steps, 2 * CHUNK), lambda i, s: (i, 0)),
                whole,
                whole,
            ],
            out_specs=pl.BlockSpec((8 // steps, C, F + 2 * CHUNK), lambda i, s: (i, 0, 0)),
            scratch_shapes=[pltpu.VMEM((F, 6 * CHUNK), bf16)],
        ),
        out_shape=jax.ShapeDtypeStruct((8, C, F + 2 * CHUNK), f32),
        compiler_params=PARAMS,
        cost_estimate=pl.CostEstimate(flops=6 * F * F * CHUNK, bytes_accessed=4 << 20, transcendentals=0),
    )(core.reshape(1).astype(jnp.int32), mine, other, mixed, mixed_other)


def after(values, others):
    flat, tree = jax.tree.flatten((values, others))
    return jax.tree.unflatten(tree, lax.optimization_barrier(flat))


def on_device(features, neighbours, tiles, weight, cotangent):
    near_at, mid_at, far_at, far_refs, place = tables(neighbours)
    own = features.T
    me_c = lax.axis_index("c")

    up = shift(own, "zh", NZ, -1)
    down = shift(own, "zh", NZ, 1)
    near = over_x(pick(pick_near_kernel, ((4, C, W),) * 3, [], near_at, own), 1)
    me_l = lax.axis_index("zl")
    cot = cotangent.T.reshape(C, NY, 2, 2, CHUNK).transpose(1, 3, 2, 0, 4).reshape(8, 2, C, CHUNK)
    cot = lax.all_to_all(cot, ("y", "c"), 0, 0, tiled=True)
    some = far_tiles(far_refs, tiles)
    (up, down), (near, cot, weight_t, some) = after((up, down), (near, cot, weight.T, some))
    weight_t = lax.all_gather(weight_t, COL, axis=0, tiled=True)
    lo, hi, *mid = pick(pick_mid_kernel, ((C, HALF * W),) * 2 + ((8, C, W),) * 3, [], mid_at, up, down)
    lo = shift(lo, "zh", NZ, -1)
    hi = shift(hi, "zh", NZ, 1)
    mid = over_x(mid, 1)
    cot_mine = lax.dynamic_index_in_dim(cot, me_l, 1, keepdims=False)
    cot_other = lax.dynamic_index_in_dim(cot, 1 - me_l, 1, keepdims=False)
    (lo, hi, mid), (cot_mine, cot_other) = after((lo, hi, mid), (cot_mine, cot_other))
    cot_other = shift(cot_other, "zl", 2, 1)
    far = pick(pick_far_kernel, ((4, C, W),) * 3, [pltpu.VMEM((C, BLK * W), f32)], far_at, lo, hi)
    far = over_x(far, 1)
    part = mix(place, own, [lo, hi, up, down, *near, *mid], tiles)
    part, cot_other = after(part, cot_other)
    mixed = mix_far(far_refs, part, far, some)

    mixed = over_col(mixed).reshape(F, CHUNK)
    rows, back = dense(weight_t, mixed, me_l, cot_mine, cot_other)
    back = over_col(back)

    rows = rows.reshape(8, 2, C, 2 * CHUNK)
    other = lax.dynamic_index_in_dim(rows, 1 - me_c, 1, keepdims=False)
    other = shift(other.reshape(8 * C, 2 * CHUNK), "c", 2, 1)
    grad = grad_part(me_c, rows, other, mixed, shift(mixed, "c", 2, 1))
    back, grad = after(back, grad)

    far = push_far(far_refs, back, some)
    far = over_x(far, -1)
    grad = lax.all_to_all(grad, ("y", "zl"), 0, 0, tiled=True)
    diag, lo, hi, up, down, *pieces = push(place, back, tiles)
    near, mid = pieces[:3], pieces[3:]
    far, mid = after(far, mid)
    mid = over_x(mid, -1)
    lo, hi = gather_sum(far_kernel, (4, 4), [pltpu.VMEM((BLK, C, W), f32)], far_at, *far, lo, hi)
    lo = shift(lo, "zh", NZ, 1)
    hi = shift(hi, "zh", NZ, -1)
    hidden = grad[:, :, F:].transpose(1, 0, 2).reshape(C, 16 * CHUNK).T
    grad = grad[:, :, :F].sum(axis=0).reshape(C, NX, W).transpose(1, 0, 2)
    (mid, lo, hi), (near, grad) = after((mid, lo, hi), (near, grad))
    up, down = gather_sum(mid_kernel, (8, 8), [], mid_at, *mid, up, down, lo, hi)
    (up, down), (near, grad) = after((up, down), (near, grad))
    up = shift(up, "zh", NZ, 1)
    down = shift(down, "zh", NZ, -1)
    near = over_x(near, -1)
    grad = lax.all_to_all(grad, "x", 0, 0, tiled=True).sum(axis=0)
    grad = grad.reshape(2, C // 2, NZ, C).transpose(2, 1, 0, 3).reshape(NZ, C // 2, 2 * C)
    grad = lax.all_to_all(grad, "zh", 0, 0, tiled=True).sum(axis=0)
    (near,) = gather_sum(near_kernel, (8,), [], near_at, *near, diag)
    grad_weight = grad.reshape(C // 2, 2, C).transpose(1, 0, 2).reshape(C, C).T
    grad_features = (near + up + down).transpose(1, 0, 2).reshape(C, BLK * W).T
    return hidden, grad_features, grad_weight


def solution(mesh):
    fine = Mesh(mesh.devices.reshape(4, 4, 4, 2, 2), DOM + COL)
    in_specs = (P(DOM, COL), P(), P(DOM, None, None, None), P(None, COL), P(DOM, COL))
    out_specs = (P(DOM, COL), P(DOM, COL), P(DOM, COL))
    return jax.shard_map(on_device, mesh=fine, in_specs=in_specs, out_specs=out_specs, check_vma=False)
```

```python
import functools

import jax
import jax.numpy as jnp
from jax import lax
from jax.experimental import pallas as pl
from jax.experimental.pallas import tpu as pltpu
from jax.sharding import Mesh
from jax.sharding import PartitionSpec as P

DOM = ("x", "zh")
COL = ("y", "zl", "c")
NX, NZ, NY = 4, 4, 4
BLK, FAN, W, C = 8, 8, 256, 64
HALF = BLK // 2
REFS = BLK * (FAN - 1)
SLOTS = 4
FAR = 60
HELD = FAR + 1
DISTANCES = (2, 1, 3)
F = 1024
CHUNK = 128
f32, bf16 = jnp.float32, jnp.bfloat16
VMEM = pl.BlockSpec(memory_space=pltpu.VMEM)
SMEM = pl.BlockSpec(memory_space=pltpu.SMEM)
ANY = pl.BlockSpec(memory_space=pl.ANY)
PARAMS = pltpu.CompilerParams(vmem_limit_bytes=58 * 2**20)
SMALL = pltpu.CompilerParams(vmem_limit_bytes=10 * 2**20)


def split(value):
    hi = value.astype(bf16)
    lo = (value - hi.astype(f32)).astype(bf16)
    return hi, lo


def tables(neighbours):
    me_x, me_z = lax.axis_index("x"), lax.axis_index("zh")
    rows = neighbours.reshape(NX, NZ, REFS)
    rows = lax.dynamic_index_in_dim(rows, me_z, 1, keepdims=False)
    rows = lax.dynamic_slice_in_dim(jnp.concatenate([rows, rows], axis=0), me_x, NX, 0)
    rows = jnp.stack([rows[s] for s in (0,) + DISTANCES])
    owner, block = rows >> 3, rows & 7
    ref = jnp.arange(REFS)
    same = (owner[:, :, None] == owner[:, None, :]) & (ref[None, :, None] > ref[None, None, :])
    rank = jnp.sum(same.astype(jnp.int32), axis=2)
    wanted = me_x * NZ + ((me_z + jnp.arange(NZ)) & (NZ - 1))
    match = (owner[None, 1:, None, :] == wanted[:, None, None, None]) & (
        rank[None, 1:, None, :] == jnp.arange(SLOTS)[None, None, :, None]
    )
    table = jnp.sum(jnp.where(match, block[None, 1:, None, :] + 1, 0), axis=3)
    e, s = ((owner[0] & 3) - me_z) & 3, (me_x - (owner[0] >> 2)) & 3
    local = jnp.where(e == 2, 0, jnp.where(e == 1, 8, 16)) + block[0]
    start = jnp.where(e == 0, 24, jnp.where(e == 2, 60, 36 + (e >> 1) * 4))
    stride = jnp.where((e & 1) == 1, 8, 4)
    turn = jnp.where(s == 3, 2, jnp.where(s == 1, 1, 0))
    place = jnp.where(s == 0, local, start + turn * stride + rank[0])
    near = table[0].reshape(12)
    mid = jnp.stack([table[1], table[3]], axis=1).reshape(24)
    far = table[2].reshape(12)
    source = ((me_x - jnp.array(DISTANCES)) & 3) * NZ + ((me_z + 2) & 3)
    match = (owner[0][None, None, :] == source[:, None, None]) & (
        rank[0][None, None, :] == jnp.arange(SLOTS)[None, :, None]
    )
    far_refs = jnp.sum(jnp.where(match, ref[None, None, :] + 1, 0), axis=2).reshape(12)
    return near, mid, far, far_refs, jnp.clip(place, 0, FAR)


def pick_slots(index_ref, sources, outs):
    per = outs[0].shape[0]
    for s in range(3):
        for slot in range(per):
            index = jnp.maximum(index_ref[s * per + slot] - 1, 0)
            outs[s][slot] = sources[slot // SLOTS][:, pl.ds(pl.multiple_of(index * W, W), W)]


def pick_near_kernel(index_ref, own_ref, *outs):
    pick_slots(index_ref, (own_ref,), outs)


def pick_mid_kernel(index_ref, up_ref, down_ref, lo_ref, hi_ref, *outs):
    lo_ref[...] = up_ref[:, : HALF * W]
    hi_ref[...] = down_ref[:, HALF * W :]
    pick_slots(index_ref, (up_ref, down_ref), outs)


def pick_far_kernel(index_ref, lo_ref, hi_ref, *refs):
    outs, held = refs[:3], refs[3]
    held[:, : HALF * W] = lo_ref[...]
    held[:, HALF * W :] = hi_ref[...]
    pick_slots(index_ref, (held,), outs)


def pick(kernel, shapes, scratch, index, *sources):
    return pl.pallas_call(
        kernel,
        out_shape=[jax.ShapeDtypeStruct(shape, f32) for shape in shapes],
        in_specs=[SMEM] + [VMEM] * len(sources),
        out_specs=[VMEM] * len(shapes),
        scratch_shapes=scratch,
        compiler_params=SMALL,
        cost_estimate=pl.CostEstimate(flops=0, bytes_accessed=2 << 20, transcendentals=0),
    )(index, *sources)


def places(refs):
    start, pairs = 0, []
    for ref in refs:
        pairs.append((pl.ds(start, ref.shape[0]), ref))
        start += ref.shape[0]
    return pairs


def mixed_kernel(place_ref, own_ref, *refs):
    sources, tiles_ref, out_ref, held, tiles, sems, tile_sems = refs[:10], *refs[10:]
    tile_copies = [pltpu.make_async_copy(tiles_ref.at[i], tiles.at[i], tile_sems.at[i]) for i in range(BLK)]
    copies, block = [], 0
    for ref in sources:
        if len(ref.shape) == 3:
            copies.append(pltpu.make_async_copy(ref, held.at[pl.ds(block, ref.shape[0])], sems.at[len(copies)]))
            block += ref.shape[0]
            continue
        for start in range(0, ref.shape[1], W):
            copies.append(pltpu.make_async_copy(ref.at[:, pl.ds(start, W)], held.at[block], sems.at[len(copies)]))
            block += 1
    for copy in copies + tile_copies:
        copy.start()
    held[FAR] = jnp.zeros((C, W), f32)
    for copy in copies:
        copy.wait()
    for i in range(BLK):
        tile_copies[i].wait()
        acc = None
        for k in range(FAN):
            block = own_ref[:, i * W : (i + 1) * W] if k == 0 else held[place_ref[i * (FAN - 1) + k - 1]]
            part = lax.dot_general(
                tiles[i, k],
                jnp.concatenate(split(block), axis=0),
                (((1,), (1,)), ((), ())),
                preferred_element_type=f32,
            )
            acc = part if acc is None else acc + part
        out_ref[i] = (acc[:, :C] + acc[:, C:]).T


def mix(place, own, sources, tiles):
    return pl.pallas_call(
        mixed_kernel,
        in_specs=[SMEM, VMEM] + [ANY] * (len(sources) + 1),
        out_specs=VMEM,
        out_shape=jax.ShapeDtypeStruct((BLK, C, W), f32),
        scratch_shapes=[
            pltpu.VMEM((HELD, C, W), f32),
            pltpu.VMEM((BLK, FAN, W, W), bf16),
            pltpu.SemaphoreType.DMA((30,)),
            pltpu.SemaphoreType.DMA((BLK,)),
        ],
        compiler_params=PARAMS,
        cost_estimate=pl.CostEstimate(flops=2 * 64 * W * W * 2 * C, bytes_accessed=13 << 20, transcendentals=0),
    )(place, own, *sources, tiles)


def far_tiles_kernel(refs_ref, tiles_ref, out_ref, sems):
    copies = []
    for slot in range(12):
        ref = jnp.maximum(refs_ref[slot] - 1, 0)
        i = ref // (FAN - 1)
        copies.append(
            pltpu.make_async_copy(tiles_ref.at[i, ref - i * (FAN - 1) + 1], out_ref.at[slot], sems.at[slot])
        )
    for copy in copies:
        copy.start()
    for copy in copies:
        copy.wait()


def far_tiles(far_refs, tiles):
    return pl.pallas_call(
        far_tiles_kernel,
        out_shape=jax.ShapeDtypeStruct((12, W, W), bf16),
        in_specs=[SMEM, ANY],
        out_specs=VMEM,
        scratch_shapes=[pltpu.SemaphoreType.DMA((12,))],
        compiler_params=PARAMS,
        cost_estimate=pl.CostEstimate(flops=0, bytes_accessed=3 << 20, transcendentals=0),
    )(far_refs, tiles)


def mix_far_kernel(refs_ref, part_ref, a_ref, b_ref, c_ref, tiles_ref, out_ref, total):
    total[...] = part_ref[...]
    for slot in range(12):
        both = jnp.concatenate(split((a_ref, b_ref, c_ref)[slot // SLOTS][slot % SLOTS]), axis=0)
        part = lax.dot_general(both, tiles_ref[slot], (((1,), (1,)), ((), ())), preferred_element_type=f32)
        ref = refs_ref[slot]
        total[jnp.maximum(ref - 1, 0) // (FAN - 1)] += jnp.where(ref > 0, part[:C] + part[C:], 0.0)
    for i in range(BLK):
        out_ref[2 * i] = total[i, :, :CHUNK]
        out_ref[2 * i + 1] = total[i, :, CHUNK:]


def mix_far(far_refs, part, far, tiles):
    return pl.pallas_call(
        mix_far_kernel,
        out_shape=jax.ShapeDtypeStruct((16, C, CHUNK), f32),
        in_specs=[SMEM] + [VMEM] * 5,
        out_specs=VMEM,
        scratch_shapes=[pltpu.VMEM((BLK, C, W), f32)],
        compiler_params=SMALL,
        cost_estimate=pl.CostEstimate(flops=2 * 12 * W * W * 2 * C, bytes_accessed=4 << 20, transcendentals=0),
    )(far_refs, part, *far, tiles)


def dense_kernel(weight_ref, mixed_ref, zl_ref, mine_ref, other_ref, rows_ref, back_ref, held, sems):
    step = F // 2
    copies = []
    for j in range(F // step):
        rows = pl.ds(j * step, step)
        copies.append(pltpu.make_async_copy(weight_ref.at[rows], held.at[rows], sems.at[j]))
    for copy in copies:
        copy.start()
    mhi, mlo = split(mixed_ref[...])
    parts = jnp.concatenate([mhi, mlo], axis=1)
    back = None
    for j, copy in enumerate(copies):
        rows = pl.ds(j * step, step)
        copy.wait()
        whi, wlo = split(held[rows])
        both = jnp.dot(whi, parts, preferred_element_type=f32)
        low = jnp.dot(wlo, mhi, preferred_element_type=f32)
        pre = both[:, :CHUNK] + (both[:, CHUNK:] + low)
        sig = jax.nn.sigmoid(pre)
        rows_ref[rows, CHUNK:] = pre * sig
        pairs = []
        for part in range(j * step // (2 * C), (j + 1) * step // (2 * C)):
            y, zl = part // 2, part % 2
            own = zl_ref[0] == zl
            pairs += [jnp.where(own, mine_ref[2 * y + c], other_ref[2 * y + c]) for c in range(2)]
        slope = jnp.concatenate(pairs, axis=0) * sig * (1.0 + pre * (1.0 - sig))
        rows_ref[rows, :CHUNK] = slope
        shi, slo = split(slope.T)
        both = jnp.dot(jnp.concatenate([shi, slo], axis=0), whi, preferred_element_type=f32)
        low = jnp.dot(shi, wlo, preferred_element_type=f32)
        part = both[:CHUNK] + (both[CHUNK:] + low)
        back = part if back is None else back + part
    back_ref[...] = back.T.reshape(16, C, CHUNK)


def dense(weight_t, mixed, me_l, cot_mine, cot_other):
    return pl.pallas_call(
        dense_kernel,
        in_specs=[ANY, VMEM, SMEM, VMEM, VMEM],
        out_specs=[VMEM, VMEM],
        out_shape=[jax.ShapeDtypeStruct((F, 2 * CHUNK), f32), jax.ShapeDtypeStruct((16, C, CHUNK), f32)],
        scratch_shapes=[pltpu.VMEM((F, F), f32), pltpu.SemaphoreType.DMA((2,))],
        compiler_params=PARAMS,
        cost_estimate=pl.CostEstimate(flops=12 * F * F * CHUNK, bytes_accessed=8 << 20, transcendentals=F * CHUNK),
    )(weight_t, mixed, me_l.reshape(1).astype(jnp.int32), cot_mine, cot_other)


def push_far_kernel(refs_ref, back_ref, tiles_ref, a_ref, b_ref, c_ref):
    for slot in range(12):
        i = jnp.maximum(refs_ref[slot] - 1, 0) // (FAN - 1)
        block = jnp.concatenate([back_ref[2 * i], back_ref[2 * i + 1]], axis=1)
        both = jnp.concatenate(split(block), axis=0)
        part = jnp.dot(both, tiles_ref[slot], preferred_element_type=f32)
        (a_ref, b_ref, c_ref)[slot // SLOTS][slot % SLOTS] = part[:C] + part[C:]


def push_far(far_refs, back, tiles):
    return pl.pallas_call(
        push_far_kernel,
        out_shape=[jax.ShapeDtypeStruct((SLOTS, C, W), f32)] * 3,
        in_specs=[SMEM, VMEM, VMEM],
        out_specs=[VMEM] * 3,
        compiler_params=SMALL,
        cost_estimate=pl.CostEstimate(flops=2 * 12 * W * W * 2 * C, bytes_accessed=4 << 20, transcendentals=0),
    )(far_refs, back, tiles)


def push_kernel(place_ref, back_ref, tiles_ref, diag_ref, *refs):
    outs, held, tiles, out_sems, tile_sems = refs[:10], *refs[10:]
    tile_copies = [pltpu.make_async_copy(tiles_ref.at[i], tiles.at[i], tile_sems.at[i]) for i in range(BLK)]
    for copy in tile_copies:
        copy.start()
    held[...] = jnp.zeros_like(held)
    for i in range(BLK):
        block = jnp.concatenate([back_ref[2 * i], back_ref[2 * i + 1]], axis=1)
        both = jnp.concatenate(split(block), axis=0)
        tile_copies[i].wait()
        for k in range(FAN):
            part = jnp.dot(both, tiles[i, k], preferred_element_type=f32)
            value = part[:C] + part[C:]
            if k == 0:
                diag_ref[i] = value
            else:
                held[place_ref[i * (FAN - 1) + k - 1]] += value
    copies = [pltpu.make_async_copy(held.at[rows], ref, out_sems.at[n]) for n, (rows, ref) in enumerate(places(outs))]
    for copy in copies:
        copy.start()
    for copy in copies:
        copy.wait()


def push(place, back, tiles):
    sizes = (4, 4, 8, 8, 4, 4, 4, 8, 8, 8)
    return pl.pallas_call(
        push_kernel,
        in_specs=[SMEM, VMEM, ANY],
        out_specs=[VMEM] + [ANY] * len(sizes),
        out_shape=[jax.ShapeDtypeStruct((n, C, W), f32) for n in (BLK,) + sizes],
        scratch_shapes=[
            pltpu.VMEM((HELD, C, W), f32),
            pltpu.VMEM((BLK, FAN, W, W), bf16),
            pltpu.SemaphoreType.DMA((len(sizes),)),
            pltpu.SemaphoreType.DMA((BLK,)),
        ],
        compiler_params=PARAMS,
        cost_estimate=pl.CostEstimate(flops=2 * 64 * W * W * 2 * C, bytes_accessed=13 << 20, transcendentals=0),
    )(place, back, tiles)


def add_slots(index_ref, got, group, out_ref):
    per = got[0].shape[0]
    for s in range(3):
        for t in range(SLOTS):
            slot = group * SLOTS + t
            index = index_ref[s * per + slot]
            out_ref[jnp.maximum(index - 1, 0)] += jnp.where(index > 0, got[s][slot], 0.0)


def far_kernel(index_ref, a_ref, b_ref, c_ref, lo_ref, hi_ref, out_lo, out_hi, total):
    total[: BLK // 2] = lo_ref[...]
    total[BLK // 2 :] = hi_ref[...]
    add_slots(index_ref, (a_ref, b_ref, c_ref), 0, total)
    out_lo[...] = total[: BLK // 2]
    out_hi[...] = total[BLK // 2 :]


def mid_kernel(index_ref, a_ref, b_ref, c_ref, up_ref, down_ref, below_ref, above_ref, out_up, out_down):
    half = BLK // 2
    out_up[:half] = up_ref[:half] + below_ref[...]
    out_up[half:] = up_ref[half:]
    out_down[:half] = down_ref[:half]
    out_down[half:] = down_ref[half:] + above_ref[...]
    add_slots(index_ref, (a_ref, b_ref, c_ref), 0, out_up)
    add_slots(index_ref, (a_ref, b_ref, c_ref), 1, out_down)


def near_kernel(index_ref, a_ref, b_ref, c_ref, diag_ref, out):
    out[...] = diag_ref[...]
    add_slots(index_ref, (a_ref, b_ref, c_ref), 0, out)


def gather_sum(kernel, shapes, scratch, index, *args):
    return pl.pallas_call(
        kernel,
        out_shape=[jax.ShapeDtypeStruct((n, C, W), f32) for n in shapes],
        in_specs=[SMEM] + [VMEM] * len(args),
        out_specs=[VMEM] * len(shapes),
        scratch_shapes=scratch,
        compiler_params=SMALL,
        cost_estimate=pl.CostEstimate(flops=12 * C * W, bytes_accessed=3 << 20, transcendentals=0),
    )(index, *args)


def shift(value, axis, size, by):
    return lax.ppermute(value, axis, [(i, (i + by) % size) for i in range(size)])


def over_x(pieces, sign):
    return [shift(piece, "x", NX, sign * s) for s, piece in zip(DISTANCES, pieces)]


def over_col(value):
    return lax.all_to_all(value, COL, 0, 0, tiled=True)


def grad_kernel(core_ref, mine_ref, other_ref, mixed_ref, far_ref, out_ref, wide):
    @pl.when(pl.program_id(0) == 0)
    def _():
        for n, ref in enumerate((mixed_ref, far_ref)):
            hi, lo = split(ref[...])
            for m, value in enumerate((hi, lo, hi)):
                start = (2 * m + n) * CHUNK
                wide[:, start : start + CHUNK] = value

    parts = out_ref.shape[0]
    mine = mine_ref[...].reshape(parts * C, 2 * CHUNK)
    other = other_ref[...]
    (ahi, alo), (bhi, blo) = split(mine[:, :CHUNK]), split(other[:, :CHUNK])
    left = jnp.concatenate([ahi, bhi, ahi, bhi, alo, blo], axis=1)
    value = lax.dot_general(left, wide[...], (((1,), (1,)), ((), ())), preferred_element_type=f32)
    out_ref[:, :, :F] = value.reshape(parts, C, F)
    low = core_ref[0] == 0
    mine, other = mine[:, CHUNK:], other[:, CHUNK:]
    out_ref[:, :, F : F + CHUNK] = jnp.where(low, mine, other).reshape(parts, C, CHUNK)
    out_ref[:, :, F + CHUNK :] = jnp.where(low, other, mine).reshape(parts, C, CHUNK)


def grad_part(core, mine, other, mixed, mixed_other):
    steps = 4
    whole = pl.BlockSpec((F, CHUNK), lambda i, s: (0, 0))
    return pl.pallas_call(
        grad_kernel,
        grid_spec=pltpu.PrefetchScalarGridSpec(
            num_scalar_prefetch=1,
            grid=(steps,),
            in_specs=[
                pl.BlockSpec((8 // steps, 1, C, 2 * CHUNK), lambda i, s: (i, s[0], 0, 0)),
                pl.BlockSpec((8 * C // steps, 2 * CHUNK), lambda i, s: (i, 0)),
                whole,
                whole,
            ],
            out_specs=pl.BlockSpec((8 // steps, C, F + 2 * CHUNK), lambda i, s: (i, 0, 0)),
            scratch_shapes=[pltpu.VMEM((F, 6 * CHUNK), bf16)],
        ),
        out_shape=jax.ShapeDtypeStruct((8, C, F + 2 * CHUNK), f32),
        compiler_params=PARAMS,
        cost_estimate=pl.CostEstimate(flops=6 * F * F * CHUNK, bytes_accessed=4 << 20, transcendentals=0),
    )(core.reshape(1).astype(jnp.int32), mine, other, mixed, mixed_other)


def after(values, others):
    flat, tree = jax.tree.flatten((values, others))
    return jax.tree.unflatten(tree, lax.optimization_barrier(flat))


def on_device(features, neighbours, tiles, weight, cotangent):
    near_at, mid_at, far_at, far_refs, place = tables(neighbours)
    own = features.T
    me_c = lax.axis_index("c")

    up = shift(own, "zh", NZ, -1)
    down = shift(own, "zh", NZ, 1)
    near = over_x(pick(pick_near_kernel, ((4, C, W),) * 3, [], near_at, own), 1)
    me_l = lax.axis_index("zl")
    cot = cotangent.T.reshape(C, NY, 2, 2, CHUNK).transpose(1, 3, 2, 0, 4).reshape(8, 2, C, CHUNK)
    cot = lax.all_to_all(cot, ("y", "c"), 0, 0, tiled=True)
    some = far_tiles(far_refs, tiles)
    (up, down), (near, cot, weight_t, some) = after((up, down), (near, cot, weight.T, some))
    weight_t = lax.all_gather(weight_t, COL, axis=0, tiled=True)
    lo, hi, *mid = pick(pick_mid_kernel, ((C, HALF * W),) * 2 + ((8, C, W),) * 3, [], mid_at, up, down)
    lo = shift(lo, "zh", NZ, -1)
    hi = shift(hi, "zh", NZ, 1)
    mid = over_x(mid, 1)
    cot_mine = lax.dynamic_index_in_dim(cot, me_l, 1, keepdims=False)
    cot_other = lax.dynamic_index_in_dim(cot, 1 - me_l, 1, keepdims=False)
    (lo, hi, mid), (cot_mine, cot_other) = after((lo, hi, mid), (cot_mine, cot_other))
    cot_other = shift(cot_other, "zl", 2, 1)
    far = pick(pick_far_kernel, ((4, C, W),) * 3, [pltpu.VMEM((C, BLK * W), f32)], far_at, lo, hi)
    far = over_x(far, 1)
    part = mix(place, own, [lo, hi, up, down, *near, *mid], tiles)
    part, cot_other = after(part, cot_other)
    mixed = mix_far(far_refs, part, far, some)

    mixed = over_col(mixed).reshape(F, CHUNK)
    rows, back = dense(weight_t, mixed, me_l, cot_mine, cot_other)
    back = over_col(back)

    rows = rows.reshape(8, 2, C, 2 * CHUNK)
    other = lax.dynamic_index_in_dim(rows, 1 - me_c, 1, keepdims=False)
    other = shift(other.reshape(8 * C, 2 * CHUNK), "c", 2, 1)
    grad = grad_part(me_c, rows, other, mixed, shift(mixed, "c", 2, 1))
    back, grad = after(back, grad)

    far = push_far(far_refs, back, some)
    far = over_x(far, -1)
    grad = lax.all_to_all(grad, ("y", "zl"), 0, 0, tiled=True)
    diag, lo, hi, up, down, *pieces = push(place, back, tiles)
    near, mid = pieces[:3], pieces[3:]
    far, mid = after(far, mid)
    mid = over_x(mid, -1)
    lo, hi = gather_sum(far_kernel, (4, 4), [pltpu.VMEM((BLK, C, W), f32)], far_at, *far, lo, hi)
    lo = shift(lo, "zh", NZ, 1)
    hi = shift(hi, "zh", NZ, -1)
    hidden = grad[:, :, F:].transpose(1, 0, 2).reshape(C, 16 * CHUNK).T
    grad = grad[:, :, :F].sum(axis=0).reshape(C, NX, W).transpose(1, 0, 2)
    (mid, lo, hi), (near, grad) = after((mid, lo, hi), (near, grad))
    up, down = gather_sum(mid_kernel, (8, 8), [], mid_at, *mid, up, down, lo, hi)
    (up, down), (near, grad) = after((up, down), (near, grad))
    up = shift(up, "zh", NZ, 1)
    down = shift(down, "zh", NZ, -1)
    near = over_x(near, -1)
    grad = lax.all_to_all(grad, "x", 0, 0, tiled=True).sum(axis=0)
    grad = grad.reshape(2, C // 2, NZ, C).transpose(2, 1, 0, 3).reshape(NZ, C // 2, 2 * C)
    grad = lax.all_to_all(grad, "zh", 0, 0, tiled=True).sum(axis=0)
    (near,) = gather_sum(near_kernel, (8,), [], near_at, *near, diag)
    grad_weight = grad.reshape(C // 2, 2, C).transpose(1, 0, 2).reshape(C, C).T
    grad_features = (near + up + down).transpose(1, 0, 2).reshape(C, BLK * W).T
    return hidden, grad_features, grad_weight


def solution(mesh):
    fine = Mesh(mesh.devices.reshape(4, 4, 4, 2, 2), DOM + COL)
    in_specs = (P(DOM, COL), P(), P(DOM, None, None, None), P(None, COL), P(DOM, COL))
    out_specs = (P(DOM, COL), P(DOM, COL), P(DOM, COL))
    return jax.shard_map(on_device, mesh=fine, in_specs=in_specs, out_specs=out_specs, check_vma=False)
```
